128 devices in a mesh: seq: 8 (over z, y_hi), tensor: 16 (over y_lo, x, core).
Axes of the slice: x: 4, y: 4 (y_hi: 2, y_lo: 2; y = y_hi * 2 + y_lo), z: 4, core: 2. Of those that a mesh axis runs over, the one named last changes fastest.
Arguments:
- queries: bfloat16 [4096, 6144], P('seq', 'tensor'), may hold values from -120 to 120
- keys: bfloat16 [4096, 6144], P('seq', 'tensor'), may hold values from -4 to 4
- values: bfloat16 [4096, 6144], P('seq', 'tensor'), may hold values from -6 to 6
- stream: bfloat16 [4096, 6144], P('seq', 'tensor'), may hold values from -160 to 160
- out_weight: bfloat16 [6144, 6144], P('tensor'), may hold values from -0.109375 to 0.109375
- norm_gain: float32 [6144], replicated, may hold values from 0.5 to 1.5
- up_weight: bfloat16 [6144, 12288], P('seq', 'tensor'), may hold values from -0.078125 to 0.078125
Outputs:
- residual_out: bfloat16 [4096, 6144], P('seq', 'tensor')
- expanded: bfloat16 [4096, 12288], P('seq', 'tensor')
The draws below stay inside these ranges and needn't reach their ends.
All inputs are finite; a program needn't handle non-finite values.
Results may differ from the reference program's by a relative error of at most 0.018.
Values may be sent and summed in bfloat16 or wider, within the bound.
A program may use at most 128 MiB of HBM per device.

```python
import math
import jax
import jax.numpy as jnp
from jax import lax

D = 6144
HEADS = 48
HD = 128
FFW = 12288
TOKENS = 4096
N_TENSOR = 16


def draw_keys(key, part):
    own_key = jax.random.fold_in(key, 3)
    shape_here = (TOKENS, HEADS * HD)
    return jnp.clip(jax.random.normal(own_key, shape_here, jnp.float32), -4.0, 4.0).astype(jnp.bfloat16)


def draw_queries(key, part):
    own_key = jax.random.fold_in(key, 5)
    shape_here = (TOKENS, HEADS * HD)
    return (2.5 * jnp.clip(jax.random.normal(own_key, shape_here, jnp.float32), -4.0, 4.0)).astype(jnp.bfloat16)


def draw_stream(key, part):
    key = jax.random.fold_in(key, 11)
    column = jnp.arange(D).astype(jnp.float32)
    rising = 3.0 ** (column / D)
    return (jnp.clip(jax.random.normal(key, (TOKENS, D), jnp.float32), -4.0, 4.0) * rising[None, :]).astype(jnp.bfloat16)


def spiked(result, rng, source, target, shards_of, factor):
    owner, partner = [(jnp.arange(result.shape[dim]) // (result.shape[dim] // shards_of)).reshape([-1 if axis == dim else 1 for axis in range(result.ndim)]) for dim in (source, target)]
    chosen = jax.random.permutation(rng, shards_of)[partner]
    strong = (owner == chosen) | (owner == (partner + shards_of // 2) % shards_of)
    return jnp.where(strong, factor * result, result)


def levels(key, shape, split, least, largest):
    level, own = 1.0, jax.random.fold_in(key, 6)
    for position, blocks in split:
        heights = jnp.exp(jax.random.uniform(jax.random.fold_in(own, position), (blocks,), jnp.float32, least / len(split), largest / len(split)))
        level = level * jnp.repeat(heights, shape[position] // blocks).reshape([-1 if axis == position else 1 for axis in range(len(shape))])
    return level


def centred(key, dims, deviation, reach, pieces=(), held_as=jnp.bfloat16):
    drawn = jax.random.normal(key, dims, jnp.float32) * deviation
    if len(pieces) > 0:
        drawn = levels(key, dims, pieces, -0.22, 0.18) * drawn
    return jnp.clip(drawn, min=-reach, max=reach).astype(held_as)


def noise_with(stream_key, extent, scale, most, pieces, heavy, kind=jnp.bfloat16):
    entries = scale * jax.random.normal(stream_key, extent, jnp.float32)
    if pieces:
        entries = entries * levels(stream_key, extent, pieces, -0.22, 0.18)
    return jnp.clip(spiked(entries, jax.random.fold_in(stream_key, 3), *heavy), -most, most).astype(kind)


def setup_inputs(seed: int = 0) -> dict:
    streams_of = jax.random.split(jax.random.key(seed), 8)
    return {
        "queries": draw_queries(jax.random.fold_in(streams_of[7], 71), 0),
        "keys": draw_keys(jax.random.fold_in(streams_of[7], 71), 0),
        "values": centred(streams_of[2], (TOKENS, HEADS * HD), 1.0, 6.0, ((0, 8), (1, 16))),
        "stream": draw_stream(jax.random.fold_in(streams_of[7], 71), 0),
        "out_weight": noise_with(streams_of[4], (HEADS * HD, D), (HEADS * HD) ** -0.5, 0.109375, ((0, 16),), (0, 1, 16, 2.0)),
        "norm_gain": jnp.clip(1.0 + 0.1 * jax.random.normal(streams_of[5], (D,), jnp.float32), 0.5, 1.5),
        "up_weight": centred(streams_of[6], (D, FFW), D ** -0.5, 0.078125, ((0, 8), (1, 16))),
    }


def reference(queries, keys, values, stream, out_weight, norm_gain, up_weight):
    softmax_scale = 1.0 / math.sqrt(HD)

    def one_head(head_index):
        offset = (head_index * HD).astype(jnp.int32)
        query_head = lax.dynamic_slice_in_dim(queries, offset, HD, 1)
        key_head = lax.dynamic_slice_in_dim(keys, offset, HD, 1)
        value_head = lax.dynamic_slice_in_dim(values, offset, HD, 1)
        scores = jnp.dot(query_head, key_head.T, preferred_element_type=jnp.float32) * softmax_scale
        row_max = lax.optimization_barrier(jnp.max(scores, axis=1, keepdims=True))
        weights = jnp.exp(scores - row_max)
        denominator = lax.optimization_barrier(jnp.sum(weights, axis=1, keepdims=True))
        product = jnp.dot(weights.astype(jnp.bfloat16), value_head, preferred_element_type=jnp.float32)
        return (product / denominator).astype(jnp.bfloat16)
    per_head = lax.map(one_head, jnp.arange(HEADS).astype(jnp.int32))
    attended = per_head.transpose(1, 0, 2).reshape(TOKENS, HEADS * HD)
    group_width = HEADS // N_TENSOR * HD
    attended_groups = attended.reshape(TOKENS, N_TENSOR, group_width).transpose(1, 0, 2)
    weight_groups = out_weight.reshape(N_TENSOR, group_width, D)

    def add_group(running, pair):
        part_rows, part_weight = pair
        partial_term = jnp.dot(part_rows, part_weight, preferred_element_type=jnp.float32).astype(jnp.bfloat16)
        return (running + partial_term.astype(jnp.float32), None)
    mixed, unused = lax.scan(add_group, jnp.zeros((TOKENS, D), jnp.float32), (attended_groups, weight_groups))
    residual_out = (stream.astype(jnp.float32) + mixed).astype(jnp.bfloat16)
    level = residual_out.astype(jnp.float32)
    inverse_rms = lax.rsqrt(lax.optimization_barrier(jnp.mean(level * level, axis=1, keepdims=True)) + 1e-06)
    normed = (level * inverse_rms * norm_gain.astype(jnp.float32)).astype(jnp.bfloat16)
    lifted = jnp.dot(normed, up_weight, preferred_element_type=jnp.float32)
    expanded = jax.nn.gelu(lifted, approximate=True).astype(jnp.bfloat16)
    return (residual_out, expanded)
```

```python
import math

import jax
import jax.numpy as jnp
from jax import lax
from jax.experimental import pallas as pl
from jax.experimental.pallas import tpu as pltpu
from jax.sharding import PartitionSpec as P

D = 6144
HD = 128
EXPONENT = math.log2(math.e) / math.sqrt(HD)
MESH = pl.DeviceIdType.MESH
BF16 = jnp.bfloat16
F32 = jnp.float32

ROWS = 512
HALF = 256
OWN = 384
WIDE = 768
SPLIT = 384


class Copies:
    def __init__(self, send, recv):
        self.send, self.recv, self.made = send, recv, {}

    def __call__(self, name, src, dst, device):
        index = len(self.made)
        self.made[name] = pltpu.make_async_remote_copy(
            src_ref=src,
            dst_ref=dst,
            send_sem=self.send.at[index],
            recv_sem=self.recv.at[index],
            device_id=device,
            device_id_type=MESH,
        )
        self.made[name].start()

    def arrive(self, *names):
        for name in names:
            self.made[name].wait_recv()

    def finish(self):
        for copy in self.made.values():
            copy.wait_send()


N_REMOTE = 96
N_LOCAL = 32


def kernel(
    q_ref, k_ref, v_ref, stream_ref, ow_ref, gain_ref, up_ref,
    residual_ref, expanded_ref,
    qb, kvb, o_out, st_out, o_in, st_in, o_own, st_own, att, owb, wb, stream_vm,
    p_far, p_plus, p_minus, p_here, r_far, r_plus, r_minus, y_out, y_in, xb, total, squares, result,
    send, recv, local_sem,
):
    s = lax.axis_index("seq")
    t = lax.axis_index("tensor")
    z, yh = s // 2, lax.rem(s, 2)
    yl, x, c = t // 8, lax.rem(t // 2, 4), lax.rem(t, 2)

    def ring(a, d):
        return lax.rem(a + d + 4, 4)

    def token_block(dz, dy):
        return ring(z, dz) * 2 + (yh if dy == 0 else 1 - yh)

    def chip(dy, dx):
        return (yl if dy == 0 else 1 - yl) * 4 + ring(x, dx)

    zp, zm = (token_block(1, 0), t), (token_block(-1, 0), t)
    yp = (token_block(0, 1), t)
    xp, xm = (s, chip(0, 1) * 2 + c), (s, chip(0, -1) * 2 + c)
    yq = (s, chip(1, 0) * 2 + c)
    cp = (s, chip(0, 0) * 2 + 1 - c)
    partners = (zp, zm, yp, xp, xm, yq, cp)

    barrier = pltpu.get_barrier_semaphore()
    for device in partners:
        pl.semaphore_signal(barrier, inc=1, device_id=device, device_id_type=MESH)

    locals_ = []

    def local(src, dst):
        copy = pltpu.make_async_copy(src, dst, local_sem.at[len(locals_)])
        copy.start()
        locals_.append(copy)
        return copy

    def head_columns(h):
        return pl.ds(h * HD, HD)

    kv_local = [
        [local(k_ref.at[:, head_columns(h)], kvb.at[h, 0, 0]), local(v_ref.at[:, head_columns(h)], kvb.at[h, 0, 1])]
        for h in range(3)
    ]
    q_local = [local(q_ref.at[:, head_columns(h)], qb.at[0, h]) for h in range(3)]
    w_local = local(up_ref, wb.at[s])
    mine = pl.ds(pl.multiple_of(c * OWN, 128), OWN)
    other = pl.ds(pl.multiple_of((1 - c) * OWN, 128), OWN)

    def feature_block(j, core):
        return pl.ds(pl.multiple_of((2 * j + core) * OWN, 128), OWN)

    ow_local = [local(ow_ref.at[:, feature_block(j, c)], owb.at[j, mine, :]) for j in range(8)]
    stream_local = local(stream_ref, stream_vm)

    pl.semaphore_wait(barrier, len(partners))
    go = Copies(send, recv)

    lower, upper = pl.ds(0, HALF), pl.ds(HALF, HALF)

    def near(h):
        go(f"n+{h}", kvb.at[h, 0], kvb.at[h, 1], zp)
        go(f"n-{h}", kvb.at[h, 0], kvb.at[h, 2], zm)

    def far(h):
        go.arrive(f"n+{h}")
        go(f"f+{h}", kvb.at[h, 1, :, lower], kvb.at[h, 3, :, lower], zp)
        go.arrive(f"n-{h}")
        go(f"f-{h}", kvb.at[h, 2, :, upper], kvb.at[h, 3, :, upper], zm)

    def attend(which, h):
        def tile(i, carry):
            rows = pl.ds(pl.multiple_of(i * HALF, HALF), HALF)
            scores = lax.dot_general(
                qb[which, h, rows, :],
                kvb[h, :, 0].reshape(4 * ROWS, HD),
                (((1,), (1,)), ((), ())),
                preferred_element_type=F32,
            )
            top = jnp.max(scores, axis=1, keepdims=True)
            weights = jnp.exp2((scores - top) * EXPONENT)
            bottom = jnp.sum(weights, axis=1, keepdims=True)
            out = jnp.dot(
                weights.astype(BF16), kvb[h, :, 1].reshape(4 * ROWS, HD), preferred_element_type=F32
            )
            out = out / bottom
            lane = lax.broadcasted_iota(jnp.int32, (HALF, HD), 1)
            both = jnp.where(lane == 0, top, bottom)
            if which == 1:
                o_out[h, rows, :] = out.astype(BF16)
                st_out[h, :, rows] = both.T[:8]
            else:
                o_own[h, rows, :] = out
                st_own[h, rows, :] = both
            return carry

        lax.fori_loop(0, 2, tile, 0)

    def give_back(h):
        go(f"o{h}", o_out.at[h], o_in.at[h], yp)
        go(f"s{h}", st_out.at[h], st_in.at[h], yp)

    for copy in kv_local[0]:
        copy.wait()
    near(0)
    for h in range(3):
        q_local[h].wait()
        go(f"q{h}", qb.at[0, h], qb.at[1, h], yp)
    for j in range(8):
        go(f"ow{j}", ow_ref.at[:, feature_block(j, 1 - c)], owb.at[j, mine, :], cp)
    for copy in kv_local[1] + kv_local[2]:
        copy.wait()
    w_local.wait()
    first, second = pl.ds(0, SPLIT), pl.ds(SPLIT, WIDE - SPLIT)
    far(0)
    near(1)
    go("wy1", wb.at[s, first], wb.at[s, first], yp)
    go("wy2", wb.at[s, second], wb.at[s, second], yp)
    go.arrive("f+0", "f-0", "q0")
    attend(1, 0)
    give_back(0)
    far(1)
    near(2)
    attend(0, 0)
    go.arrive("f+1", "f-1", "q1")
    attend(1, 1)
    give_back(1)
    far(2)
    attend(0, 1)
    go.arrive("f+2", "f-2", "q2")
    go("wz2+", wb.at[s, second], wb.at[s, second], zp)
    go("wz2-", wb.at[s, second], wb.at[s, second], zm)
    go("wz1+", wb.at[s, first], wb.at[s, first], zp)
    go("wz1-", wb.at[s, first], wb.at[s, first], zm)
    attend(1, 2)
    give_back(2)
    attend(0, 2)

    for h in range(3):
        go.arrive(f"o{h}", f"s{h}")
        theirs = jnp.concatenate([st_in[h]] * 16, axis=0).T
        top1, sum1 = st_own[h][:, 0:1], st_own[h][:, 1:2]
        top2, sum2 = theirs[:, 0:1], theirs[:, 1:2]
        top = jnp.maximum(top1, top2)
        w1 = sum1 * jnp.exp2((top1 - top) * EXPONENT)
        w2 = sum2 * jnp.exp2((top2 - top) * EXPONENT)
        scale = 1.0 / (w1 + w2)
        merged = (w1 * scale) * o_own[h] + (w2 * scale) * o_in[h].astype(F32)
        att[:, pl.ds(pl.multiple_of(c * OWN + h * HD, HD), HD)] = merged.astype(BF16)
    go("att", att.at[:, mine], att.at[:, mine], cp)
    for copy in ow_local:
        copy.wait()
    go.arrive(*[f"ow{j}" for j in range(8)])
    go.arrive("att")

    def project(dy, dx):
        return jnp.dot(att[...], owb[chip(dy, dx)], preferred_element_type=F32)

    for dy in (1, 0):
        p_far[dy] = project(dy, 2).astype(BF16)
        go(f"far+{dy}", p_far.at[dy, lower], r_far.at[dy, lower], xp)
        go(f"far-{dy}", p_far.at[dy, upper], r_far.at[dy, upper], xm)
        p_plus[dy] = project(dy, 1)
        p_minus[dy] = project(dy, -1)
        y_out[0, dy, upper, :] = p_plus[dy, upper, :].astype(BF16)
        y_out[1, dy, lower, :] = p_minus[dy, lower, :].astype(BF16)
        go(f"early+{dy}", y_out.at[0, dy, upper], r_plus.at[dy, upper], xp)
        go(f"early-{dy}", y_out.at[1, dy, lower], r_minus.at[dy, lower], xm)
    for dy in (1, 0):
        p_here[dy] = project(dy, 0)
    for dy in (1, 0):
        go.arrive(f"far+{dy}")
        y_out[0, dy, lower, :] = (p_plus[dy, lower, :] + r_far[dy, lower, :].astype(F32)).astype(BF16)
        go(f"late+{dy}", y_out.at[0, dy, lower], r_plus.at[dy, lower], xp)
        go.arrive(f"far-{dy}")
        y_out[1, dy, upper, :] = (p_minus[dy, upper, :] + r_far[dy, upper, :].astype(F32)).astype(BF16)
        go(f"late-{dy}", y_out.at[1, dy, upper], r_minus.at[dy, upper], xm)
    before, after, across = token_block(-1, 0), token_block(1, 0), token_block(2, 0)
    opposite = token_block(0, 1)
    go.arrive("wz2+")
    go("wq1", wb.at[before, second], wb.at[before, second], yp)
    go.arrive("wz2-")
    go("wf2", wb.at[after, second], wb.at[after, second], zm)
    go("wq2", wb.at[after, second], wb.at[after, second], yp)

    def near_sum(dy):
        go.arrive(f"early+{dy}", f"early-{dy}", f"late+{dy}", f"late-{dy}")
        return p_here[dy] + r_plus[dy].astype(F32) + r_minus[dy].astype(F32)

    y_in[0] = near_sum(1).astype(BF16)
    go("rows", y_in.at[0], y_in.at[1], yq)
    go.arrive("wz1+")
    go("wf1", wb.at[before, first], wb.at[before, first], zp)
    go.arrive("wz1-", "wy1")
    go("wp+", wb.at[opposite, first], wb.at[opposite, first], zp)
    go("wp-", wb.at[opposite, first], wb.at[opposite, first], zm)
    stream_local.wait()
    here = near_sum(0) + stream_vm[...].astype(F32)
    go.arrive("rows")
    own = chip(0, 0)
    xb[own, :, mine] = (here + y_in[1].astype(F32)).astype(BF16)
    residual_out = local(xb.at[own, :, mine], residual_ref)

    go("xc", xb.at[own, :, mine], xb.at[own, :, mine], cp)
    go("xy", xb.at[own, :, mine], xb.at[own, :, mine], yq)
    go("x+0", xb.at[own, :, mine], xb.at[own, :, mine], xp)
    go("x-0", xb.at[own, :, mine], xb.at[own, :, mine], xm)

    def pass_on(dy):
        left, right, far_chip = chip(dy, -1), chip(dy, 1), chip(dy, 2)
        go.arrive(f"x+{dy}")
        go(f"xf+{dy}", xb.at[left, lower, mine], xb.at[left, lower, mine], xp)
        go(f"xc+{dy}", xb.at[left, :, mine], xb.at[left, :, mine], cp)
        go.arrive(f"x-{dy}")
        go(f"xf-{dy}", xb.at[right, upper, mine], xb.at[right, upper, mine], xm)
        go(f"xc-{dy}", xb.at[right, :, mine], xb.at[right, :, mine], cp)

    def pass_far(dy):
        far_chip = chip(dy, 2)
        go.arrive(f"xf+{dy}", f"xf-{dy}")
        go(f"xcf{dy}", xb.at[far_chip, :, mine], xb.at[far_chip, :, mine], cp)

    def expand(j, start=False):
        gain = gain_ref[:, pl.ds(pl.multiple_of(j * WIDE, 128), WIDE)]
        level = xb[j].astype(F32)
        sums = jnp.sum(level * level, axis=1, keepdims=True)
        scaled = (level * gain).astype(BF16)
        product = jnp.dot(scaled, wb[j], preferred_element_type=F32)
        if start:
            squares[...] = jnp.broadcast_to(sums, (ROWS, 128))
            total[...] = product
        else:
            squares[...] += jnp.broadcast_to(sums, (ROWS, 128))
            total[...] += product

    far_opposite, before_opposite, after_opposite = token_block(2, 1), token_block(-1, 1), token_block(1, 1)
    q1, q2 = pl.ds(0, SPLIT // 2), pl.ds(SPLIT // 2, SPLIT // 2)
    pass_on(0)
    go.arrive("xy")
    other_chip = chip(1, 0)
    go("x+1", xb.at[other_chip, :, mine], xb.at[other_chip, :, mine], xp)
    go("x-1", xb.at[other_chip, :, mine], xb.at[other_chip, :, mine], xm)
    go("xcy", xb.at[other_chip, :, mine], xb.at[other_chip, :, mine], cp)
    go.arrive("wf2")
    go("wq3", wb.at[across, second], wb.at[across, second], yp)
    go.arrive("wp+")
    go("wpf+", wb.at[before_opposite, q1], wb.at[before_opposite, q1], zp)
    go.arrive("wp-")
    go("wpf-", wb.at[after_opposite, q2], wb.at[after_opposite, q2], zm)
    pass_far(0)
    pass_on(1)
    go.arrive("wy2", "wf1", "wpf+", "wpf-", "wq1", "wq2", "wq3")
    go.arrive("xc")
    expand(own, start=True)
    go.arrive("xc+0")
    expand(chip(0, -1))
    go.arrive("xc-0")
    expand(chip(0, 1))
    go.arrive("xcy")
    expand(chip(1, 0))
    go.arrive("xcf0")
    expand(chip(0, 2))
    go.arrive("xc+1")
    expand(chip(1, -1))
    go.arrive("xc-1")
    expand(chip(1, 1))
    pass_far(1)
    go.arrive("xcf1")
    expand(chip(1, 2))

    inverse = lax.rsqrt(squares[:, 0:1] * (1.0 / D) + 1e-6)
    result[...] = jax.nn.gelu(total[...] * inverse, approximate=True).astype(BF16)
    expanded_out = local(result, expanded_ref)
    go.finish()
    residual_out.wait()
    expanded_out.wait()


def body(queries, keys, values, stream, out_weight, norm_gain, up_weight):
    anywhere = pl.BlockSpec(memory_space=pl.ANY)
    vmem = pl.BlockSpec(memory_space=pltpu.VMEM)
    return pl.pallas_call(
        kernel,
        out_shape=(
            jax.ShapeDtypeStruct((ROWS, OWN), BF16),
            jax.ShapeDtypeStruct((ROWS, WIDE), BF16),
        ),
        in_specs=[anywhere, anywhere, anywhere, anywhere, anywhere, vmem, anywhere],
        out_specs=(anywhere, anywhere),
        scratch_shapes=[
            pltpu.VMEM((2, 3, ROWS, HD), BF16),
            pltpu.VMEM((3, 4, 2, ROWS, HD), BF16),
            pltpu.VMEM((3, ROWS, HD), BF16),
            pltpu.VMEM((3, 8, ROWS), F32),
            pltpu.VMEM((3, ROWS, HD), BF16),
            pltpu.VMEM((3, 8, ROWS), F32),
            pltpu.VMEM((3, ROWS, HD), F32),
            pltpu.VMEM((3, ROWS, HD), F32),
            pltpu.VMEM((ROWS, WIDE), BF16),
            pltpu.VMEM((8, WIDE, OWN), BF16),
            pltpu.VMEM((8, WIDE, WIDE), BF16),
            pltpu.VMEM((ROWS, OWN), BF16),
            pltpu.VMEM((2, ROWS, OWN), BF16),
            pltpu.VMEM((2, ROWS, OWN), F32),
            pltpu.VMEM((2, ROWS, OWN), F32),
            pltpu.VMEM((2, ROWS, OWN), F32),
            pltpu.VMEM((2, ROWS, OWN), BF16),
            pltpu.VMEM((2, ROWS, OWN), BF16),
            pltpu.VMEM((2, ROWS, OWN), BF16),
            pltpu.VMEM((2, 2, ROWS, OWN), BF16),
            pltpu.VMEM((2, ROWS, OWN), BF16),
            pltpu.VMEM((8, ROWS, WIDE), BF16),
            pltpu.VMEM((ROWS, WIDE), F32),
            pltpu.VMEM((ROWS, 128), F32),
            pltpu.VMEM((ROWS, WIDE), BF16),
            pltpu.SemaphoreType.DMA((N_REMOTE,)),
            pltpu.SemaphoreType.DMA((N_REMOTE,)),
            pltpu.SemaphoreType.DMA((N_LOCAL,)),
        ],
        compiler_params=pltpu.CompilerParams(
            collective_id=0, has_side_effects=True, vmem_limit_bytes=60 * 2**20
        ),
        cost_estimate=pl.CostEstimate(flops=10_500_000_000, bytes_accessed=12_000_000, transcendentals=6_300_000),
    )(queries, keys, values, stream, out_weight, norm_gain.reshape(1, D), up_weight)


def solution(mesh):
    in_specs = (
        P("seq", "tensor"),
        P("seq", "tensor"),
        P("seq", "tensor"),
        P("seq", "tensor"),
        P("tensor", None),
        P(),
        P("seq", "tensor"),
    )
    out_specs = (P("seq", "tensor"), P("seq", "tensor"))
    return jax.shard_map(body, mesh=mesh, in_specs=in_specs, out_specs=out_specs, check_vma=False)
```

```python
import math

import jax
import jax.numpy as jnp
from jax import lax
from jax.experimental import pallas as pl
from jax.experimental.pallas import tpu as pltpu
from jax.sharding import PartitionSpec as P

D = 6144
HD = 128
EXPONENT = math.log2(math.e) / math.sqrt(HD)
MESH = pl.DeviceIdType.MESH
BF16 = jnp.bfloat16
F32 = jnp.float32

ROWS = 512
HALF = 256
OWN = 384
WIDE = 768
SPLIT = 512


class Copies:
    def __init__(self, send, recv):
        self.send, self.recv, self.made = send, recv, {}

    def __call__(self, name, src, dst, device):
        index = len(self.made)
        self.made[name] = pltpu.make_async_remote_copy(
            src_ref=src,
            dst_ref=dst,
            send_sem=self.send.at[index],
            recv_sem=self.recv.at[index],
            device_id=device,
            device_id_type=MESH,
        )
        self.made[name].start()

    def arrive(self, *names):
        for name in names:
            self.made[name].wait_recv()

    def finish(self):
        for copy in self.made.values():
            copy.wait_send()


N_REMOTE = 96
N_LOCAL = 32


def kernel(
    q_ref, k_ref, v_ref, stream_ref, ow_ref, gain_ref, up_ref,
    residual_ref, expanded_ref,
    qb, kvb, o_out, st_out, o_in, st_in, o_own, st_own, att, owb, wb, stream_vm,
    p_far, p_plus, p_minus, p_here, r_far, r_plus, r_minus, y_out, y_in, xb, total, squares, result,
    send, recv, local_sem,
):
    s = lax.axis_index("seq")
    t = lax.axis_index("tensor")
    z, yh = s // 2, lax.rem(s, 2)
    yl, x, c = t // 8, lax.rem(t // 2, 4), lax.rem(t, 2)

    def ring(a, d):
        return lax.rem(a + d + 4, 4)

    def token_block(dz, dy):
        return ring(z, dz) * 2 + (yh if dy == 0 else 1 - yh)

    def chip(dy, dx):
        return (yl if dy == 0 else 1 - yl) * 4 + ring(x, dx)

    zp, zm = (token_block(1, 0), t), (token_block(-1, 0), t)
    yp = (token_block(0, 1), t)
    xp, xm = (s, chip(0, 1) * 2 + c), (s, chip(0, -1) * 2 + c)
    yq = (s, chip(1, 0) * 2 + c)
    cp = (s, chip(0, 0) * 2 + 1 - c)
    partners = (zp, zm, yp, xp, xm, yq, cp)

    barrier = pltpu.get_barrier_semaphore()
    for device in partners:
        pl.semaphore_signal(barrier, inc=1, device_id=device, device_id_type=MESH)

    locals_ = []

    def local(src, dst):
        copy = pltpu.make_async_copy(src, dst, local_sem.at[len(locals_)])
        copy.start()
        locals_.append(copy)
        return copy

    def head_columns(h):
        return pl.ds(h * HD, HD)

    kv_local = [
        [local(k_ref.at[:, head_columns(h)], kvb.at[h, 0, 0]), local(v_ref.at[:, head_columns(h)], kvb.at[h, 0, 1])]
        for h in range(3)
    ]
    q_local = [local(q_ref.at[:, head_columns(h)], qb.at[0, h]) for h in range(3)]
    w_local = local(up_ref, wb.at[s])
    mine = pl.ds(pl.multiple_of(c * OWN, 128), OWN)
    other = pl.ds(pl.multiple_of((1 - c) * OWN, 128), OWN)

    def feature_block(j, core):
        return pl.ds(pl.multiple_of((2 * j + core) * OWN, 128), OWN)

    ow_local = [local(ow_ref.at[:, feature_block(j, c)], owb.at[j, mine, :]) for j in range(8)]
    stream_local = local(stream_ref, stream_vm)

    pl.semaphore_wait(barrier, len(partners))
    go = Copies(send, recv)

    lower, upper = pl.ds(0, HALF), pl.ds(HALF, HALF)

    def near(h):
        go(f"n+{h}", kvb.at[h, 0], kvb.at[h, 1], zp)
        go(f"n-{h}", kvb.at[h, 0], kvb.at[h, 2], zm)

    def far(h):
        go.arrive(f"n+{h}")
        go(f"f+{h}", kvb.at[h, 1, :, lower], kvb.at[h, 3, :, lower], zp)
        go.arrive(f"n-{h}")
        go(f"f-{h}", kvb.at[h, 2, :, upper], kvb.at[h, 3, :, upper], zm)

    def attend(which, h):
        def tile(i, carry):
            rows = pl.ds(pl.multiple_of(i * HALF, HALF), HALF)
            scores = lax.dot_general(
                qb[which, h, rows, :],
                kvb[h, :, 0].reshape(4 * ROWS, HD),
                (((1,), (1,)), ((), ())),
                preferred_element_type=F32,
            )
            top = jnp.max(scores, axis=1, keepdims=True)
            weights = jnp.exp2((scores - top) * EXPONENT)
            bottom = jnp.sum(weights, axis=1, keepdims=True)
            out = jnp.dot(
                weights.astype(BF16), kvb[h, :, 1].reshape(4 * ROWS, HD), preferred_element_type=F32
            )
            out = out / bottom
            lane = lax.broadcasted_iota(jnp.int32, (HALF, HD), 1)
            both = jnp.where(lane == 0, top, bottom)
            if which == 1:
                o_out[h, rows, :] = out.astype(BF16)
                st_out[h, :, rows] = both.T[:8]
            else:
                o_own[h, rows, :] = out
                st_own[h, rows, :] = both
            return carry

        lax.fori_loop(0, 2, tile, 0)

    def give_back(h):
        go(f"o{h}", o_out.at[h], o_in.at[h], yp)
        go(f"s{h}", st_out.at[h], st_in.at[h], yp)

    for copy in kv_local[0]:
        copy.wait()
    near(0)
    for copy in kv_local[1]:
        copy.wait()
    near(1)
    for h in range(3):
        q_local[h].wait()
        go(f"q{h}", qb.at[0, h], qb.at[1, h], yp)
    for j in range(8):
        go(f"ow{j}", ow_ref.at[:, feature_block(j, 1 - c)], owb.at[j, mine, :], cp)
    for copy in kv_local[2]:
        copy.wait()
    w_local.wait()
    first, second = pl.ds(0, SPLIT), pl.ds(SPLIT, WIDE - SPLIT)
    own_rows = token_block(0, 0)

    def cross(i):
        rows = pl.ds(i * 128, 128)
        go(f"wy{i}", wb.at[own_rows, rows], wb.at[own_rows, rows], yp)

    cross(0)
    cross(1)
    far(0)
    near(2)
    far(1)
    go.arrive("f+0", "f-0", "q0")
    attend(1, 0)
    give_back(0)
    cross(2)
    cross(3)
    attend(0, 0)
    far(2)
    go("wz2+", wb.at[own_rows, second], wb.at[own_rows, second], zp)
    go("wz2-", wb.at[own_rows, second], wb.at[own_rows, second], zm)
    go("wz1+", wb.at[own_rows, first], wb.at[own_rows, first], zp)
    go("wz1-", wb.at[own_rows, first], wb.at[own_rows, first], zm)
    go.arrive("f+1", "f-1", "q1")
    attend(1, 1)
    give_back(1)
    attend(0, 1)
    go.arrive("f+2", "f-2", "q2")
    attend(1, 2)
    give_back(2)
    cross(4)
    cross(5)
    attend(0, 2)

    def merge(h):
        theirs = jnp.concatenate([st_in[h]] * 16, axis=0).T
        top1, sum1 = st_own[h][:, 0:1], st_own[h][:, 1:2]
        top2, sum2 = theirs[:, 0:1], theirs[:, 1:2]
        top = jnp.maximum(top1, top2)
        w1 = sum1 * jnp.exp2((top1 - top) * EXPONENT)
        w2 = sum2 * jnp.exp2((top2 - top) * EXPONENT)
        scale = 1.0 / (w1 + w2)
        merged = (w1 * scale) * o_own[h] + (w2 * scale) * o_in[h].astype(F32)
        att[:, pl.ds(pl.multiple_of(c * OWN + h * HD, HD), HD)] = merged.astype(BF16)

    for h in range(3):
        go.arrive(f"o{h}", f"s{h}")
        merge(h)
        columns = pl.ds(pl.multiple_of(c * OWN + h * HD, HD), HD)
        go(f"att{h}", att.at[:, columns], att.at[:, columns], cp)
    for copy in ow_local:
        copy.wait()
    go.arrive(*[f"ow{j}" for j in range(8)])
    before, after, across = token_block(-1, 0), token_block(1, 0), token_block(2, 0)
    opposite = token_block(0, 1)
    before_opposite, after_opposite = token_block(-1, 1), token_block(1, 1)
    go.arrive("wz2+")
    go("wq1", wb.at[before, second], wb.at[before, second], yp)
    go.arrive("att0", "att1", "att2")

    def project(dy, dx):
        return jnp.dot(att[...], owb[chip(dy, dx)], preferred_element_type=F32)

    def send_far(dy):
        go(f"far+{dy}", p_far.at[dy, lower], r_far.at[dy, lower], xp)
        go(f"far-{dy}", p_far.at[dy, upper], r_far.at[dy, upper], xm)

    def send_early(dy):
        go(f"early+{dy}", y_out.at[0, dy, upper], r_plus.at[dy, upper], xp)
        go(f"early-{dy}", y_out.at[1, dy, lower], r_minus.at[dy, lower], xm)

    def send_late(dy):
        go.arrive(f"far+{dy}")
        y_out[0, dy, lower, :] = (p_plus[dy, lower, :] + r_far[dy, lower, :].astype(F32)).astype(BF16)
        go(f"late+{dy}", y_out.at[0, dy, lower], r_plus.at[dy, lower], xp)
        go.arrive(f"far-{dy}")
        y_out[1, dy, upper, :] = (p_minus[dy, upper, :] + r_far[dy, upper, :].astype(F32)).astype(BF16)
        go(f"late-{dy}", y_out.at[1, dy, upper], r_minus.at[dy, upper], xm)

    def near_blocks(dy):
        p_plus[dy] = project(dy, 1)
        p_minus[dy] = project(dy, -1)
        y_out[0, dy, upper, :] = p_plus[dy, upper, :].astype(BF16)
        y_out[1, dy, lower, :] = p_minus[dy, lower, :].astype(BF16)

    def near_sum(dy):
        go.arrive(f"early+{dy}", f"early-{dy}", f"late+{dy}", f"late-{dy}")
        return p_here[dy] + r_plus[dy].astype(F32) + r_minus[dy].astype(F32)

    p_far[1] = project(1, 2).astype(BF16)
    send_far(1)
    near_blocks(1)
    send_early(1)
    p_far[0] = project(0, 2).astype(BF16)
    near_blocks(0)
    send_late(1)
    send_far(0)
    send_early(0)
    p_here[1] = project(1, 0)
    p_here[0] = project(0, 0)
    go.arrive("wz2-")
    go("wf2", wb.at[after, second], wb.at[after, second], zm)
    go.arrive("wy0", "wy1", "wy2", "wy3")
    go("wp+", wb.at[opposite, first], wb.at[opposite, first], zp)
    go("wp-", wb.at[opposite, first], wb.at[opposite, first], zm)
    y_in[0] = near_sum(1).astype(BF16)
    go("rows", y_in.at[0], y_in.at[1], yq)
    half1, half2 = pl.ds(SPLIT, 128), pl.ds(SPLIT + 128, 128)
    go("wq2a", wb.at[after, half1], wb.at[after, half1], yp)
    send_late(0)
    rows1, rows2 = pl.ds(0, WIDE // 2), pl.ds(WIDE // 2, SPLIT - WIDE // 2)
    go.arrive("wz1+")
    go("wf1", wb.at[before, rows1], wb.at[before, rows1], zp)
    go.arrive("wz1-")
    go("wf3", wb.at[after, rows2], wb.at[after, rows2], zm)
    stream_local.wait()
    here = near_sum(0) + stream_vm[...].astype(F32)
    go.arrive("rows")
    own = chip(0, 0)
    xb[own, :, mine] = (here + y_in[1].astype(F32)).astype(BF16)

    def block(j, rows=slice(None)):
        return xb.at[j, rows, mine]

    def spread(dy):
        j = chip(dy, 0)
        go(f"x+{dy}a", block(j, lower), block(j, lower), xp)
        go(f"x-{dy}a", block(j, upper), block(j, upper), xm)
        go(f"x+{dy}b", block(j, upper), block(j, upper), xp)
        go(f"x-{dy}b", block(j, lower), block(j, lower), xm)

    def pass_on(dy):
        left, right = chip(dy, -1), chip(dy, 1)
        go.arrive(f"x+{dy}a")
        go(f"xf+{dy}", block(left, lower), block(left, lower), xp)
        go.arrive(f"x-{dy}a")
        go(f"xf-{dy}", block(right, upper), block(right, upper), xm)

    def pass_core(dy):
        left, right = chip(dy, -1), chip(dy, 1)
        go.arrive(f"x+{dy}b")
        go(f"xc+{dy}", block(left), block(left), cp)
        go.arrive(f"x-{dy}b")
        go(f"xc-{dy}", block(right), block(right), cp)

    def pass_far(dy):
        j = chip(dy, 2)
        go.arrive(f"xf+{dy}", f"xf-{dy}")
        go(f"xcf{dy}", block(j), block(j), cp)

    def expand(j, start=False):
        gain = gain_ref[:, pl.ds(pl.multiple_of(j * WIDE, 128), WIDE)]
        level = xb[j].astype(F32)
        sums = jnp.sum(level * level, axis=1, keepdims=True)
        scaled = (level * gain).astype(BF16)
        product = jnp.dot(scaled, wb[j], preferred_element_type=F32)
        if start:
            squares[...] = jnp.broadcast_to(sums, (ROWS, 128))
            total[...] = product
        else:
            squares[...] += jnp.broadcast_to(sums, (ROWS, 128))
            total[...] += product

    spread(0)
    go("xy", block(own), block(own), yq)
    go("xc", block(own), block(own), cp)
    residual_out = local(block(own), residual_ref)
    go("wq2b", wb.at[after, half2], wb.at[after, half2], yp)
    go.arrive("wf2")
    go("wq3", wb.at[across, second], wb.at[across, second], yp)
    pass_on(0)
    pass_core(0)
    go.arrive("xy")
    spread(1)
    other_chip = chip(1, 0)
    go("xcy", block(other_chip), block(other_chip), cp)
    q1, q2 = pl.ds(0, SPLIT // 2), pl.ds(SPLIT // 2, SPLIT // 2)
    go.arrive("wp+")
    go("wpf+", wb.at[before_opposite, q1], wb.at[before_opposite, q1], zp)
    go.arrive("wp-")
    go("wpf-", wb.at[after_opposite, q2], wb.at[after_opposite, q2], zm)
    pass_far(0)
    pass_on(1)
    pass_core(1)
    go.arrive("wy4", "wy5", "wf1", "wf3", "wq1", "wq2a", "wq2b", "wpf+", "wpf-", "wq3")
    go.arrive("xc")
    expand(own, start=True)
    go.arrive("xc+0")
    expand(chip(0, -1))
    go.arrive("xc-0")
    expand(chip(0, 1))
    go.arrive("xcy")
    expand(chip(1, 0))
    go.arrive("xcf0")
    expand(chip(0, 2))
    go.arrive("xc+1")
    expand(chip(1, -1))
    go.arrive("xc-1")
    expand(chip(1, 1))
    pass_far(1)
    go.arrive("xcf1")
    expand(chip(1, 2))

    outs = []
    for rows in (lower, upper):
        inverse = lax.rsqrt(squares[rows, 0:1] * (1.0 / D) + 1e-6)
        result[rows] = jax.nn.gelu(total[rows] * inverse, approximate=True).astype(BF16)
        outs.append(local(result.at[rows], expanded_ref.at[rows]))
    go.finish()
    residual_out.wait()
    for copy in outs:
        copy.wait()


def body(queries, keys, values, stream, out_weight, norm_gain, up_weight):
    anywhere = pl.BlockSpec(memory_space=pl.ANY)
    vmem = pl.BlockSpec(memory_space=pltpu.VMEM)
    return pl.pallas_call(
        kernel,
        out_shape=(
            jax.ShapeDtypeStruct((ROWS, OWN), BF16),
            jax.ShapeDtypeStruct((ROWS, WIDE), BF16),
        ),
        in_specs=[anywhere, anywhere, anywhere, anywhere, anywhere, vmem, anywhere],
        out_specs=(anywhere, anywhere),
        scratch_shapes=[
            pltpu.VMEM((2, 3, ROWS, HD), BF16),
            pltpu.VMEM((3, 4, 2, ROWS, HD), BF16),
            pltpu.VMEM((3, ROWS, HD), BF16),
            pltpu.VMEM((3, 8, ROWS), F32),
            pltpu.VMEM((3, ROWS, HD), BF16),
            pltpu.VMEM((3, 8, ROWS), F32),
            pltpu.VMEM((3, ROWS, HD), F32),
            pltpu.VMEM((3, ROWS, HD), F32),
            pltpu.VMEM((ROWS, WIDE), BF16),
            pltpu.VMEM((8, WIDE, OWN), BF16),
            pltpu.VMEM((8, WIDE, WIDE), BF16),
            pltpu.VMEM((ROWS, OWN), BF16),
            pltpu.VMEM((2, ROWS, OWN), BF16),
            pltpu.VMEM((2, ROWS, OWN), F32),
            pltpu.VMEM((2, ROWS, OWN), F32),
            pltpu.VMEM((2, ROWS, OWN), F32),
            pltpu.VMEM((2, ROWS, OWN), BF16),
            pltpu.VMEM((2, ROWS, OWN), BF16),
            pltpu.VMEM((2, ROWS, OWN), BF16),
            pltpu.VMEM((2, 2, ROWS, OWN), BF16),
            pltpu.VMEM((2, ROWS, OWN), BF16),
            pltpu.VMEM((8, ROWS, WIDE), BF16),
            pltpu.VMEM((ROWS, WIDE), F32),
            pltpu.VMEM((ROWS, 128), F32),
            pltpu.VMEM((ROWS, WIDE), BF16),
            pltpu.SemaphoreType.DMA((N_REMOTE,)),
            pltpu.SemaphoreType.DMA((N_REMOTE,)),
            pltpu.SemaphoreType.DMA((N_LOCAL,)),
        ],
        compiler_params=pltpu.CompilerParams(
            collective_id=0, has_side_effects=True, vmem_limit_bytes=60 * 2**20
        ),
        cost_estimate=pl.CostEstimate(flops=10_500_000_000, bytes_accessed=12_000_000, transcendentals=6_300_000),
    )(queries, keys, values, stream, out_weight, norm_gain.reshape(1, D), up_weight)


def solution(mesh):
    in_specs = (
        P("seq", "tensor"),
        P("seq", "tensor"),
        P("seq", "tensor"),
        P("seq", "tensor"),
        P("tensor", None),
        P(),
        P("seq", "tensor"),
    )
    out_specs = (P("seq", "tensor"), P("seq", "tensor"))
    return jax.shard_map(body, mesh=mesh, in_specs=in_specs, out_specs=out_specs, check_vma=False)
```

```python
import math

import jax
import jax.numpy as jnp
from jax import lax
from jax.experimental import pallas as pl
from jax.experimental.pallas import tpu as pltpu
from jax.sharding import PartitionSpec as P

D = 6144
HD = 128
EXPONENT = math.log2(math.e) / math.sqrt(HD)
MESH = pl.DeviceIdType.MESH
BF16 = jnp.bfloat16
F32 = jnp.float32

ROWS = 512
HALF = 256
OWN = 384
WIDE = 768
SPLIT = 512


class Copies:
    def __init__(self, send, recv):
        self.send, self.recv = send, recv
        self.made, self.slots, self.groups = {}, {}, {}
        self.free, self.used = [], 0

    def __call__(self, name, src, dst, device, group=None):
        if not self.free:
            self.free.append(self.used)
            self.used += 1
        self.slots[name] = slot = self.free.pop()
        index = self.groups.setdefault(group or name, len(self.groups))
        self.made[name] = copy = pltpu.make_async_remote_copy(
            src_ref=src,
            dst_ref=dst,
            send_sem=self.send.at[slot],
            recv_sem=self.recv.at[index],
            device_id=device,
            device_id_type=MESH,
        )
        copy.start()

    def arrive(self, *names):
        for name in names:
            self.made[name].wait_recv()

    def arrive_all(self, group, ref, device):
        pltpu.make_async_remote_copy(
            src_ref=ref,
            dst_ref=ref,
            send_sem=self.send.at[0],
            recv_sem=self.recv.at[self.groups[group]],
            device_id=device,
            device_id_type=MESH,
        ).wait_recv()

    def drain(self, *names):
        for name in names or tuple(self.slots):
            self.made[name].wait_send()
            self.free.append(self.slots.pop(name))


N_SEND = 47
N_RECV = 66
N_LOCAL = 8


def kernel(
    q_ref, k_ref, v_ref, stream_ref, ow_ref, gain_ref, up_ref,
    residual_ref, expanded_ref,
    qb, kvb, o_out, st_out, o_in, st_in, o_part, st_part, att, owb, wb, stream_vm,
    p_far, p_out, p_plus, p_minus, p_here, r_far, r_plus, r_minus, y_out, y_in, xb, xg, total, squares,
    send, recv, local_sem,
):
    s = lax.axis_index("seq")
    t = lax.axis_index("tensor")
    z, yh = s // 2, lax.rem(s, 2)
    yl, x, c = t // 8, lax.rem(t // 2, 4), lax.rem(t, 2)

    def ring(a, d):
        return lax.rem(a + d + 4, 4)

    def token_block(dz, dy):
        return ring(z, dz) * 2 + (yh if dy == 0 else 1 - yh)

    def chip(dy, dx):
        return (yl if dy == 0 else 1 - yl) * 4 + ring(x, dx)

    zp, zm = (token_block(1, 0), t), (token_block(-1, 0), t)
    yp = (token_block(0, 1), t)
    xp, xm = (s, chip(0, 1) * 2 + c), (s, chip(0, -1) * 2 + c)
    yq = (s, chip(1, 0) * 2 + c)
    cp = (s, chip(0, 0) * 2 + 1 - c)
    partners = (zp, zm, yp, xp, xm, yq, cp)

    barrier = pltpu.get_barrier_semaphore()
    for device in partners:
        pl.semaphore_signal(barrier, inc=1, device_id=device, device_id_type=MESH)

    def local(index, *pairs):
        for src, dst in pairs:
            pltpu.make_async_copy(src, dst, local_sem.at[index]).start()

    def landed(index, ref):
        pltpu.make_async_copy(ref, ref, local_sem.at[index]).wait()

    def head_columns(h):
        return pl.ds(h * HD, HD)

    for h in range(3):
        local(
            h,
            (k_ref.at[:, head_columns(h)], kvb.at[h, 0, 0]),
            (v_ref.at[:, head_columns(h)], kvb.at[h, 0, 1]),
        )
    local(3, *[(q_ref.at[:, head_columns(h)], qb.at[0, h]) for h in range(3)])
    local(4, (up_ref, wb.at[s]))
    mine = pl.ds(pl.multiple_of(c * OWN, 128), OWN)

    def feature_block(j, core):
        return pl.ds(pl.multiple_of((2 * j + core) * OWN, 128), OWN)

    local(5, *[(ow_ref.at[:, :, feature_block(j, c)], owb.at[j, :, c]) for j in range(8)])
    local(6, (stream_ref, stream_vm))

    def greeted():
        pl.semaphore_wait(barrier, len(partners))

    greeted()
    go = Copies(send, recv)

    lower, upper = pl.ds(0, HALF), pl.ds(HALF, HALF)

    def near(h):
        go(f"n+{h}", kvb.at[h, 0], kvb.at[h, 1], zp)
        go(f"n-{h}", kvb.at[h, 0], kvb.at[h, 2], zm)

    def far(h):
        go.arrive(f"n+{h}")
        go(f"f+{h}", kvb.at[h, 1, :, lower], kvb.at[h, 3, :, lower], zp, f"f{h}")
        go.arrive(f"n-{h}")
        go(f"f-{h}", kvb.at[h, 2, :, upper], kvb.at[h, 3, :, upper], zm, f"f{h}")

    def scores_of(which, h, rows, slots):
        keys = kvb[h, slots, 0].reshape(-1, HD)
        return lax.dot_general(
            qb[which, h, rows, :], keys, (((1,), (1,)), ((), ())), preferred_element_type=F32
        )

    lane = lax.broadcasted_iota(jnp.int32, (HALF, HD), 1)

    def attend_near(which, h):
        def tile(i, carry):
            rows = pl.ds(pl.multiple_of(i * HALF, HALF), HALF)
            slots = slice(0, 3)
            scores = scores_of(which, h, rows, slots)
            top = jnp.max(scores, axis=1, keepdims=True)
            weights = jnp.exp2((scores - top) * EXPONENT)
            bottom = jnp.sum(weights, axis=1, keepdims=True)
            o_part[which, h, rows, :] = jnp.dot(
                weights.astype(BF16), kvb[h, slots, 1].reshape(-1, HD), preferred_element_type=F32
            )
            st_part[which, h, rows, :] = jnp.where(lane == 0, top, bottom)
            return carry

        lax.fori_loop(0, 2, tile, 0)

    def attend_far(which, h, halves=None):
        def tile(i, carry):
            rows = pl.ds(i * HALF if isinstance(i, int) else pl.multiple_of(i * HALF, HALF), HALF)
            slots = slice(3, 4)
            scores = scores_of(which, h, rows, slots)
            stats = st_part[which, h, rows, :]
            top_near, bottom_near = stats[:, 0:1], stats[:, 1:2]
            top = jnp.maximum(top_near, jnp.max(scores, axis=1, keepdims=True))
            weights = jnp.exp2((scores - top) * EXPONENT)
            decay = jnp.exp2((top_near - top) * EXPONENT)
            bottom = bottom_near * decay + jnp.sum(weights, axis=1, keepdims=True)
            out = jnp.dot(weights.astype(BF16), kvb[h, slots, 1].reshape(-1, HD), preferred_element_type=F32)
            out = (o_part[which, h, rows, :] * decay + out) / bottom
            both = jnp.where(lane == 0, top, bottom)
            if which == 1:
                o_out[h, rows, :] = out.astype(BF16)
                st_out[h, :, rows] = both.T[:8]
            else:
                o_part[0, h, rows, :] = out
                st_part[0, h, rows, :] = both
            return carry

        if halves is None:
            lax.fori_loop(0, 2, tile, 0)
        else:
            tile(halves, 0)

    def give_back(h, part="", rows=slice(None)):
        go(f"s{h}{part}", st_out.at[h, :, rows], st_in.at[h, :, rows], yp)
        go(f"o{h}{part}", o_out.at[h, rows], o_in.at[h, rows], yp)

    landed(0, kvb.at[0, 0])
    near(0)
    landed(1, kvb.at[1, 0])
    near(1)
    landed(3, qb.at[0])
    for h in range(3):
        go(f"q{h}", qb.at[0, h], qb.at[1, h], yp)
    for j in range(8):
        go(f"ow{j}", ow_ref.at[:, :, feature_block(j, 1 - c)], owb.at[j, :, c], cp, "ow")
    landed(2, kvb.at[2, 0])
    landed(4, wb.at[s])
    first, second = pl.ds(0, SPLIT), pl.ds(SPLIT, WIDE - SPLIT)
    own_rows = token_block(0, 0)

    def cross(i, n=2):
        rows = pl.ds(i * 64, n * 64)
        go(f"wy{i}", wb.at[own_rows, rows], wb.at[own_rows, rows], yp, "wy1" if i < SPLIT // 64 else "wy2")

    cross(0)
    cross(2)
    far(0)
    near(2)
    go.arrive("q0")
    attend_near(1, 0)
    attend_near(0, 0)
    far(1)
    go.arrive("q1")
    attend_near(1, 1)
    attend_near(0, 1)
    go.arrive_all("f0", kvb.at[0, 3], zp)
    attend_far(1, 0)
    give_back(0)
    cross(4)
    attend_far(0, 0)
    far(2)
    go("wz2+", wb.at[own_rows, second], wb.at[own_rows, second], zp)
    go("wz2-", wb.at[own_rows, second], wb.at[own_rows, second], zm)
    go("wz1+", wb.at[own_rows, first], wb.at[own_rows, first], zp)
    go("wz1-", wb.at[own_rows, first], wb.at[own_rows, first], zm)
    go.arrive("q2")
    attend_near(1, 2)
    attend_near(0, 2)
    go.arrive_all("f1", kvb.at[1, 3], zp)
    attend_far(1, 1)
    give_back(1)
    attend_far(0, 1)
    go.arrive_all("f2", kvb.at[2, 3], zp)
    attend_far(1, 2, 0)
    give_back(2, "a", lower)
    attend_far(1, 2, 1)
    give_back(2, "b", upper)
    cross(6)
    cross(8)
    cross(10)
    attend_far(0, 2)

    def merge(h, rows):
        theirs = jnp.concatenate([st_in[h, :, rows]] * 16, axis=0).T
        ours = st_part[0, h, rows, :]
        top1, sum1 = ours[:, 0:1], ours[:, 1:2]
        top2, sum2 = theirs[:, 0:1], theirs[:, 1:2]
        top = jnp.maximum(top1, top2)
        w1 = sum1 * jnp.exp2((top1 - top) * EXPONENT)
        w2 = sum2 * jnp.exp2((top2 - top) * EXPONENT)
        scale = 1.0 / (w1 + w2)
        merged = (w1 * scale) * o_part[0, h, rows, :] + (w2 * scale) * o_in[h, rows, :].astype(F32)
        att[h, rows, own_half] = merged.astype(BF16)

    own_half = pl.ds(pl.multiple_of(c * HD, HD), HD)
    whole = pl.ds(0, ROWS)
    for h in range(2):
        go.arrive(f"s{h}", f"o{h}")
        merge(h, whole)
        go(f"att{h}", att.at[h, :, own_half], att.at[h, :, own_half], cp, "att")
    go.drain(*[f"{kind}{h}" for kind in ("n+", "n-", "f+", "f-", "q") for h in range(3)], *[f"ow{j}" for j in range(8)])
    landed(5, owb.at[:, :, c])
    go.arrive_all("ow", owb.at[:, :, 1 - c], cp)
    go.arrive_all("att", att.at[0:2, :, own_half], cp)

    def project_two(dy, dx):
        return jnp.dot(
            jnp.concatenate([att[0], att[1]], axis=1),
            owb[chip(dy, dx), 0:2].reshape(4 * HD, OWN),
            preferred_element_type=F32,
        )

    def project_last(dy, dx, rows):
        return jnp.dot(
            att[2, rows, :], owb[chip(dy, dx), 2].reshape(2 * HD, OWN), preferred_element_type=F32
        )

    p_far[1] = project_two(1, 2)
    p_plus[1] = project_two(1, 1)
    p_minus[1] = project_two(1, -1)
    for part, rows in (("a", lower), ("b", upper)):
        go.arrive(f"s2{part}", f"o2{part}")
        merge(2, rows)
        go(f"att2{part}", att.at[2, rows, own_half], att.at[2, rows, own_half], cp)
    p_far[0] = project_two(0, 2)
    before, after, across = token_block(-1, 0), token_block(1, 0), token_block(2, 0)
    opposite = token_block(0, 1)
    before_opposite, after_opposite, across_opposite = token_block(-1, 1), token_block(1, 1), token_block(2, 1)

    def send_far(dy, rows):
        p_out[dy, rows, :] = (p_far[dy, rows, :] + project_last(dy, 2, rows)).astype(BF16)
        if rows is lower:
            go(f"far+{dy}", p_out.at[dy, rows], r_far.at[dy, rows], xp)
        else:
            go(f"far-{dy}", p_out.at[dy, rows], r_far.at[dy, rows], xm)

    def near_blocks(dy):
        p_plus[dy] += project_last(dy, 1, whole)
        y_out[0, dy, upper, :] = p_plus[dy, upper, :].astype(BF16)
        p_minus[dy] += project_last(dy, -1, whole)
        y_out[1, dy, lower, :] = p_minus[dy, lower, :].astype(BF16)

    def send_early(dy):
        go(f"early+{dy}", y_out.at[0, dy, upper], r_plus.at[dy, upper], xp, f"plus{dy}")
        go(f"early-{dy}", y_out.at[1, dy, lower], r_minus.at[dy, lower], xm, f"minus{dy}")

    def send_late(dy):
        go.arrive(f"far+{dy}")
        y_out[0, dy, lower, :] = (p_plus[dy, lower, :] + r_far[dy, lower, :].astype(F32)).astype(BF16)
        go(f"late+{dy}", y_out.at[0, dy, lower], r_plus.at[dy, lower], xp, f"plus{dy}")
        go.arrive(f"far-{dy}")
        y_out[1, dy, upper, :] = (p_minus[dy, upper, :] + r_far[dy, upper, :].astype(F32)).astype(BF16)
        go(f"late-{dy}", y_out.at[1, dy, upper], r_minus.at[dy, upper], xm, f"minus{dy}")

    def near_sum(dy):
        go.arrive_all(f"plus{dy}", r_plus.at[dy], xp)
        go.arrive_all(f"minus{dy}", r_minus.at[dy], xm)
        return p_here[dy] + r_plus[dy].astype(F32) + r_minus[dy].astype(F32)

    go.arrive("att2a")
    send_far(1, lower)
    go.arrive("att2b")
    send_far(1, upper)
    near_blocks(1)
    send_early(1)
    go.arrive("wz2+")
    go("wq1", wb.at[before, second], wb.at[before, second], yp)
    go.arrive("wz2-")
    go("wf2", wb.at[after, second], wb.at[after, second], zm)
    p_plus[0] = project_two(0, 1)
    p_minus[0] = project_two(0, -1)
    near_blocks(0)
    send_late(1)
    send_far(0, lower)
    send_far(0, upper)
    send_early(0)
    for dy in (1, 0):
        p_here[dy] = project_two(dy, 0) + project_last(dy, 0, whole)
    go.arrive_all("wy1", wb.at[opposite, first], yp)
    go("wp+", wb.at[opposite, first], wb.at[opposite, first], zp)
    go("wp-", wb.at[opposite, first], wb.at[opposite, first], zm)
    y_in[0] = near_sum(1).astype(BF16)
    go("rows", y_in.at[0], y_in.at[1], yq)
    half1, half2 = pl.ds(SPLIT, 128), pl.ds(SPLIT + 128, 128)
    go("wq2a", wb.at[after, half1], wb.at[after, half1], yp, "wq2")
    send_late(0)
    rows1, rows2 = pl.ds(0, WIDE // 2), pl.ds(WIDE // 2, SPLIT - WIDE // 2)
    go.arrive("wz1+")
    go("wf1", wb.at[before, rows1], wb.at[before, rows1], zp, "wf")
    go.arrive("wz1-")
    go("wf3", wb.at[after, rows2], wb.at[after, rows2], zm, "wf")
    landed(6, stream_vm)
    here = near_sum(0) + stream_vm[...].astype(F32)
    go.arrive("rows")
    own = chip(0, 0)
    residual = (here + y_in[1].astype(F32)).astype(BF16)
    xb[own, :, mine] = residual
    residual_ref[...] = residual

    def block(j, rows=slice(None)):
        return xb.at[j, rows, mine]

    def spread(dy):
        j = chip(dy, 0)
        go(f"x+{dy}a", block(j, lower), block(j, lower), xp)
        go(f"x-{dy}a", block(j, upper), block(j, upper), xm)
        go(f"x+{dy}b", block(j, upper), block(j, upper), xp)
        go(f"x-{dy}b", block(j, lower), block(j, lower), xm)

    def pass_on(dy):
        left, right = chip(dy, -1), chip(dy, 1)
        go.arrive(f"x+{dy}a")
        go(f"xf+{dy}", block(left, lower), block(left, lower), xp, f"xf{dy}")
        go.arrive(f"x-{dy}a")
        go(f"xf-{dy}", block(right, upper), block(right, upper), xm, f"xf{dy}")

    def pass_core(dy):
        left, right = chip(dy, -1), chip(dy, 1)
        go.arrive(f"x+{dy}b")
        go(f"xc+{dy}", block(left), block(left), cp)
        go.arrive(f"x-{dy}b")
        go(f"xc-{dy}", block(right), block(right), cp)

    def pass_far(dy):
        j = chip(dy, 2)
        go.arrive_all(f"xf{dy}", block(j), xp)
        go(f"xcf{dy}", block(j), block(j), cp)

    def prepare(j, start=False):
        gain = gain_ref[:, pl.ds(pl.multiple_of(j * WIDE, 128), WIDE)]
        level = xb[j].astype(F32)
        xg[j] = (level * gain).astype(BF16)
        level = level * level
        sums = level[:, 0:128]
        for k in range(1, WIDE // 128):
            sums = sums + level[:, k * 128 : (k + 1) * 128]
        squares[...] = sums if start else squares[...] + sums

    def expand(j, start=False):
        product = jnp.dot(xg[j], wb[j], preferred_element_type=F32)
        total[...] = product if start else total[...] + product

    go.drain(*[f"{kind}{sign}{dy}" for kind in ("far", "early", "late") for sign in "+-" for dy in (0, 1)])
    go.drain(*"s0 o0 s1 o1 s2a o2a s2b o2b att0 att1 att2a att2b wy0 wy2 wy4 wy6 wy8 wy10".split())
    go.drain("wz2+", "wz2-", "wz1+", "wz1-")
    spread(0)
    go("xy", block(own), block(own), yq)
    go("xc", block(own), block(own), cp)
    go("wq2b", wb.at[after, half2], wb.at[after, half2], yp, "wq2")
    go.arrive("wf2")
    go("wq3", wb.at[across, second], wb.at[across, second], yp)
    go.arrive("xc")
    prepare(own, start=True)
    pass_on(0)
    pass_core(0)
    go.arrive("xy")
    spread(1)
    other_chip = chip(1, 0)
    go("xcy", block(other_chip), block(other_chip), cp)
    q1, q2 = pl.ds(0, SPLIT // 2), pl.ds(SPLIT // 2, SPLIT // 2)
    go.arrive("wp+")
    go("wpf+", wb.at[before_opposite, q1], wb.at[before_opposite, q1], zp, "wpf")
    go.arrive("wp-")
    go("wpf-", wb.at[after_opposite, q2], wb.at[after_opposite, q2], zm, "wpf")
    go.arrive("xc+0")
    prepare(chip(0, -1))
    go.arrive("xc-0")
    prepare(chip(0, 1))
    pass_far(0)
    go.arrive("xcy")
    prepare(other_chip)
    pass_on(1)
    go.arrive("xcf0")
    prepare(chip(0, 2))
    go.arrive_all("wf", wb.at[across, first], zp)
    same = lax.rem(x + yh, 2)
    rest = 1 - same
    expand(chip(0, same), start=True)
    expand(chip(0, same + 2))
    go.arrive_all("wy2", wb.at[opposite, second], yp)
    go.arrive("wq1", "wq3")
    go.arrive_all("wq2", wb.at[after_opposite, second], yp)
    go.arrive_all("wpf", wb.at[across_opposite, first], zp)
    expand(chip(0, rest))
    pass_core(1)
    expand(chip(0, rest + 2))
    go.arrive("xc+1")
    prepare(chip(1, -1))
    go.arrive("xc-1")
    prepare(chip(1, 1))
    expand(other_chip)
    expand(chip(1, 1))
    pass_far(1)
    expand(chip(1, -1))
    go.arrive("xcf1")
    prepare(chip(1, 2))
    expand(chip(1, 2))

    for rows in (lower, upper):
        inverse = lax.rsqrt(jnp.sum(squares[rows], axis=1, keepdims=True) * (1.0 / D) + 1e-6)
        expanded_ref[rows] = jax.nn.gelu(total[rows] * inverse, approximate=True).astype(BF16)
    go.drain()
    assert go.used <= N_SEND and len(go.groups) <= N_RECV, (go.used, len(go.groups))


def body(queries, keys, values, stream, out_weight, norm_gain, up_weight):
    anywhere = pl.BlockSpec(memory_space=pl.ANY)
    vmem = pl.BlockSpec(memory_space=pltpu.VMEM)
    return pl.pallas_call(
        kernel,
        out_shape=(
            pltpu.VMEM((ROWS, OWN), BF16),
            pltpu.VMEM((ROWS, WIDE), BF16),
        ),
        in_specs=[anywhere, anywhere, anywhere, anywhere, anywhere, vmem, anywhere],
        out_specs=(vmem, vmem),
        scratch_shapes=[
            pltpu.VMEM((2, 3, ROWS, HD), BF16),
            pltpu.VMEM((3, 4, 2, ROWS, HD), BF16),
            pltpu.VMEM((3, ROWS, HD), BF16),
            pltpu.VMEM((3, 8, ROWS), F32),
            pltpu.VMEM((3, ROWS, HD), BF16),
            pltpu.VMEM((3, 8, ROWS), F32),
            pltpu.VMEM((2, 3, ROWS, HD), F32),
            pltpu.VMEM((2, 3, ROWS, HD), F32),
            pltpu.VMEM((3, ROWS, 2 * HD), BF16),
            pltpu.VMEM((8, 3, 2, HD, OWN), BF16),
            pltpu.VMEM((8, WIDE, WIDE), BF16),
            pltpu.VMEM((ROWS, OWN), BF16),
            pltpu.VMEM((2, ROWS, OWN), F32),
            pltpu.VMEM((2, ROWS, OWN), BF16),
            pltpu.VMEM((2, ROWS, OWN), F32),
            pltpu.VMEM((2, ROWS, OWN), F32),
            pltpu.VMEM((2, ROWS, OWN), F32),
            pltpu.VMEM((2, ROWS, OWN), BF16),
            pltpu.VMEM((2, ROWS, OWN), BF16),
            pltpu.VMEM((2, ROWS, OWN), BF16),
            pltpu.VMEM((2, 2, ROWS, OWN), BF16),
            pltpu.VMEM((2, ROWS, OWN), BF16),
            pltpu.VMEM((8, ROWS, WIDE), BF16),
            pltpu.VMEM((8, ROWS, WIDE), BF16),
            pltpu.VMEM((ROWS, WIDE), F32),
            pltpu.VMEM((ROWS, 128), F32),
            pltpu.SemaphoreType.DMA((N_SEND,)),
            pltpu.SemaphoreType.DMA((N_RECV,)),
            pltpu.SemaphoreType.DMA((N_LOCAL,)),
        ],
        compiler_params=pltpu.CompilerParams(
            collective_id=0, has_side_effects=True, vmem_limit_bytes=53 * 2**20
        ),
        cost_estimate=pl.CostEstimate(flops=10_500_000_000, bytes_accessed=12_000_000, transcendentals=6_300_000),
    )(queries, keys, values, stream, out_weight.reshape(3, HD, D), norm_gain.reshape(1, D), up_weight)


def solution(mesh):
    in_specs = (
        P("seq", "tensor"),
        P("seq", "tensor"),
        P("seq", "tensor"),
        P("seq", "tensor"),
        P("tensor", None),
        P(),
        P("seq", "tensor"),
    )
    out_specs = (P("seq", "tensor"), P("seq", "tensor"))
    return jax.shard_map(body, mesh=mesh, in_specs=in_specs, out_specs=out_specs, check_vma=False)
```

```python
import math

import jax
import jax.numpy as jnp
from jax import lax
from jax.experimental import pallas as pl
from jax.experimental.pallas import tpu as pltpu
from jax.sharding import PartitionSpec as P

D = 6144
HD = 128
EXPONENT = math.log2(math.e) / math.sqrt(HD)
MESH = pl.DeviceIdType.MESH
BF16 = jnp.bfloat16
F32 = jnp.float32

ROWS = 512
HALF = 256
QUARTER = 128
OWN = 384
WIDE = 768
SPLIT = 512


class Copies:
    def __init__(self, send, recv):
        self.send, self.recv = send, recv
        self.made, self.slots, self.groups = {}, {}, {}
        self.free, self.used = [], 0

    def __call__(self, name, src, dst, device, group=None):
        if not self.free:
            self.free.append(self.used)
            self.used += 1
        self.slots[name] = slot = self.free.pop()
        index = self.groups.setdefault(group or name, len(self.groups))
        self.made[name] = copy = pltpu.make_async_remote_copy(
            src_ref=src,
            dst_ref=dst,
            send_sem=self.send.at[slot],
            recv_sem=self.recv.at[index],
            device_id=device,
            device_id_type=MESH,
        )
        copy.start()

    def arrive(self, *names):
        for name in names:
            self.made[name].wait_recv()

    def arrive_all(self, group, ref, device):
        pltpu.make_async_remote_copy(
            src_ref=ref,
            dst_ref=ref,
            send_sem=self.send.at[0],
            recv_sem=self.recv.at[self.groups[group]],
            device_id=device,
            device_id_type=MESH,
        ).wait_recv()

    def drain(self, *names):
        for name in names or tuple(self.slots):
            self.made[name].wait_send()
            self.free.append(self.slots.pop(name))


N_SEND = 53
N_RECV = 75
N_LOCAL = 8


def kernel(
    q_ref, k_ref, v_ref, stream_ref, ow_ref, gain_ref, up_ref,
    residual_ref, expanded_ref,
    qb, kvb, o_out, st_out, o_in, st_in, o_part, st_part, att, owb, wb, stream_vm,
    p_far, p_out, p_plus, p_minus, p_here, r_far, r_plus, r_minus, y_out, y_in, xb, xg, total, squares,
    send, recv, local_sem,
):
    s = lax.axis_index("seq")
    t = lax.axis_index("tensor")
    z, yh = s // 2, lax.rem(s, 2)
    yl, x, c = t // 8, lax.rem(t // 2, 4), lax.rem(t, 2)

    def ring(a, d):
        return lax.rem(a + d + 4, 4)

    def token_block(dz, dy):
        return ring(z, dz) * 2 + (yh if dy == 0 else 1 - yh)

    def chip(dy, dx):
        return (yl if dy == 0 else 1 - yl) * 4 + ring(x, dx)

    zp, zm = (token_block(1, 0), t), (token_block(-1, 0), t)
    yp = (token_block(0, 1), t)
    xp, xm = (s, chip(0, 1) * 2 + c), (s, chip(0, -1) * 2 + c)
    yq = (s, chip(1, 0) * 2 + c)
    cp = (s, chip(0, 0) * 2 + 1 - c)
    partners = (zp, zm, yp, xp, xm, yq, cp)

    barrier = pltpu.get_barrier_semaphore()
    for device in partners:
        pl.semaphore_signal(barrier, inc=1, device_id=device, device_id_type=MESH)

    def local(index, *pairs):
        for src, dst in pairs:
            pltpu.make_async_copy(src, dst, local_sem.at[index]).start()

    def landed(index, ref):
        pltpu.make_async_copy(ref, ref, local_sem.at[index]).wait()

    def head_columns(h):
        return pl.ds(h * HD, HD)

    for h in range(3):
        local(
            h,
            (k_ref.at[:, head_columns(h)], kvb.at[h, 0, 0]),
            (v_ref.at[:, head_columns(h)], kvb.at[h, 0, 1]),
        )
    local(3, *[(q_ref.at[:, head_columns(h)], qb.at[0, h]) for h in range(3)])
    local(4, (up_ref, wb.at[s]))
    mine = pl.ds(pl.multiple_of(c * OWN, 128), OWN)

    def feature_block(j, core):
        return pl.ds(pl.multiple_of((2 * j + core) * OWN, 128), OWN)

    local(5, *[(ow_ref.at[:, :, feature_block(j, c)], owb.at[j, :, c]) for j in range(8)])
    local(6, (stream_ref, stream_vm))

    def greeted():
        pl.semaphore_wait(barrier, len(partners))

    greeted()
    go = Copies(send, recv)

    lower, upper = pl.ds(0, HALF), pl.ds(HALF, HALF)

    def near(h):
        go(f"n+{h}", kvb.at[h, 0], kvb.at[h, 1], zp)
        go(f"n-{h}", kvb.at[h, 0], kvb.at[h, 2], zm)

    def far(h):
        go.arrive(f"n+{h}")
        go(f"f+{h}", kvb.at[h, 1, :, lower], kvb.at[h, 3, :, lower], zp, f"f{h}")
        go.arrive(f"n-{h}")
        go(f"f-{h}", kvb.at[h, 2, :, upper], kvb.at[h, 3, :, upper], zm, f"f{h}")

    def scores_of(which, h, rows, slots):
        keys = kvb[h, slots, 0].reshape(-1, HD)
        return lax.dot_general(
            qb[which, h, rows, :], keys, (((1,), (1,)), ((), ())), preferred_element_type=F32
        )

    lane = lax.broadcasted_iota(jnp.int32, (HALF, HD), 1)

    def attend_near(which, h):
        def tile(i, carry):
            rows = pl.ds(pl.multiple_of(i * HALF, HALF), HALF)
            slots = slice(0, 3)
            scores = scores_of(which, h, rows, slots)
            top = jnp.max(scores, axis=1, keepdims=True)
            weights = jnp.exp2((scores - top) * EXPONENT)
            bottom = jnp.sum(weights, axis=1, keepdims=True)
            o_part[which, h, rows, :] = jnp.dot(
                weights.astype(BF16), kvb[h, slots, 1].reshape(-1, HD), preferred_element_type=F32
            )
            st_part[which, h, rows, :] = jnp.where(lane == 0, top, bottom)
            return carry

        lax.fori_loop(0, 2, tile, 0)

    def attend_far(which, h, halves=None):
        def tile(i, carry):
            rows = pl.ds(i * HALF if isinstance(i, int) else pl.multiple_of(i * HALF, HALF), HALF)
            slots = slice(3, 4)
            scores = scores_of(which, h, rows, slots)
            stats = st_part[which, h, rows, :]
            top_near, bottom_near = stats[:, 0:1], stats[:, 1:2]
            top = jnp.maximum(top_near, jnp.max(scores, axis=1, keepdims=True))
            weights = jnp.exp2((scores - top) * EXPONENT)
            decay = jnp.exp2((top_near - top) * EXPONENT)
            bottom = bottom_near * decay + jnp.sum(weights, axis=1, keepdims=True)
            out = jnp.dot(weights.astype(BF16), kvb[h, slots, 1].reshape(-1, HD), preferred_element_type=F32)
            out = (o_part[which, h, rows, :] * decay + out) / bottom
            both = jnp.where(lane == 0, top, bottom)
            if which == 1:
                o_out[h, rows, :] = out.astype(BF16)
                st_out[h, :, rows] = both.T[:8]
            else:
                o_part[0, h, rows, :] = out
                st_part[0, h, rows, :] = both
            return carry

        if halves is None:
            lax.fori_loop(0, 2, tile, 0)
        else:
            tile(halves, 0)

    def give_back(h, part="", rows=slice(None)):
        go(f"s{h}{part}", st_out.at[h, :, rows], st_in.at[h, :, rows], yp)
        go(f"o{h}{part}", o_out.at[h, rows], o_in.at[h, rows], yp)

    landed(0, kvb.at[0, 0])
    near(0)
    landed(1, kvb.at[1, 0])
    near(1)
    landed(3, qb.at[0])
    for h in range(3):
        go(f"q{h}", qb.at[0, h], qb.at[1, h], yp)
    for j in range(8):
        go(f"ow{j}", ow_ref.at[:, :, feature_block(j, 1 - c)], owb.at[j, :, c], cp, "ow")
    landed(2, kvb.at[2, 0])
    landed(4, wb.at[s])
    first, second = pl.ds(0, SPLIT), pl.ds(SPLIT, WIDE - SPLIT)
    own_rows = token_block(0, 0)

    def cross(i, n=2):
        rows = pl.ds(i * 64, n * 64)
        go(f"wy{i}", wb.at[own_rows, rows], wb.at[own_rows, rows], yp, "wy1" if i < SPLIT // 64 else "wy2")

    cross(0)
    cross(2)
    far(0)
    near(2)
    go.arrive("q0")
    attend_near(1, 0)
    attend_near(0, 0)
    far(1)
    go.arrive("q1")
    attend_near(1, 1)
    attend_near(0, 1)
    go.arrive_all("f0", kvb.at[0, 3], zp)
    attend_far(1, 0)
    give_back(0)
    cross(4)
    attend_far(0, 0)
    far(2)
    go("wz2+", wb.at[own_rows, second], wb.at[own_rows, second], zp)
    go("wz2-", wb.at[own_rows, second], wb.at[own_rows, second], zm)
    go("wz1+", wb.at[own_rows, first], wb.at[own_rows, first], zp)
    go("wz1-", wb.at[own_rows, first], wb.at[own_rows, first], zm)
    go.arrive("q2")
    attend_near(1, 2)
    attend_near(0, 2)
    go.arrive_all("f1", kvb.at[1, 3], zp)
    attend_far(1, 1)
    give_back(1)
    go.arrive_all("f2", kvb.at[2, 3], zp)
    attend_far(1, 2, 0)
    give_back(2, "a", lower)
    attend_far(1, 2, 1)
    give_back(2, "b", upper)
    cross(6)
    cross(8)
    cross(10)
    attend_far(0, 1)
    attend_far(0, 2)

    def merge(h, rows):
        theirs = jnp.concatenate([st_in[h, :, rows]] * 16, axis=0).T
        ours = st_part[0, h, rows, :]
        top1, sum1 = ours[:, 0:1], ours[:, 1:2]
        top2, sum2 = theirs[:, 0:1], theirs[:, 1:2]
        top = jnp.maximum(top1, top2)
        w1 = sum1 * jnp.exp2((top1 - top) * EXPONENT)
        w2 = sum2 * jnp.exp2((top2 - top) * EXPONENT)
        scale = 1.0 / (w1 + w2)
        merged = (w1 * scale) * o_part[0, h, rows, :] + (w2 * scale) * o_in[h, rows, :].astype(F32)
        att[h, rows, own_half] = merged.astype(BF16)

    own_half = pl.ds(pl.multiple_of(c * HD, HD), HD)
    whole = pl.ds(0, ROWS)
    for h in range(2):
        go.arrive(f"s{h}", f"o{h}")
        merge(h, whole)
        go(f"att{h}", att.at[h, :, own_half], att.at[h, :, own_half], cp, "att")
    go.drain(*[f"{kind}{h}" for kind in ("n+", "n-") for h in range(2)], "f+0", "f-0", "q0", "q1", "q2")
    go.drain(*[f"ow{j}" for j in range(8)])
    for part, rows in (("a", lower), ("b", upper)):
        go.arrive(f"s2{part}", f"o2{part}")
        merge(2, rows)
        go(f"att2{part}", att.at[2, rows, own_half], att.at[2, rows, own_half], cp)
    landed(5, owb.at[:, :, c])
    go.arrive_all("ow", owb.at[:, :, 1 - c], cp)
    go.arrive_all("att", att.at[0:2, :, own_half], cp)

    def project_two(dy, dx):
        return jnp.dot(
            jnp.concatenate([att[0], att[1]], axis=1),
            owb[chip(dy, dx), 0:2].reshape(4 * HD, OWN),
            preferred_element_type=F32,
        )

    def project_last(dy, dx, rows):
        return jnp.dot(
            att[2, rows, :], owb[chip(dy, dx), 2].reshape(2 * HD, OWN), preferred_element_type=F32
        )

    before, after, across = token_block(-1, 0), token_block(1, 0), token_block(2, 0)
    opposite = token_block(0, 1)
    before_opposite, after_opposite, across_opposite = token_block(-1, 1), token_block(1, 1), token_block(2, 1)

    def quarters(a):
        return a.reshape(2, 2, QUARTER, OWN)

    def send_far(dy, half):
        go(f"far+{dy}{half}", p_out.at[dy, half, 0], r_far.at[dy, half, 0], xp, f"far+{dy}")
        go(f"far-{dy}{half}", p_out.at[dy, half, 1], r_far.at[dy, half, 1], xm, f"far-{dy}")

    def far_block(dy, rows, half):
        out = p_far[dy, rows, :] + project_last(dy, 2, rows)
        p_out[dy, half] = out.astype(BF16).reshape(2, QUARTER, OWN)

    def near_blocks(dy):
        p_plus[dy] = quarters(project_two(dy, 1) + project_last(dy, 1, whole))
        y_out[0, dy, :, 1] = p_plus[dy, :, 1].astype(BF16)
        p_minus[dy] = quarters(project_two(dy, -1) + project_last(dy, -1, whole))
        y_out[1, dy, :, 0] = p_minus[dy, :, 0].astype(BF16)

    def send_early(dy):
        go(f"early+{dy}", y_out.at[0, dy, :, 1], r_plus.at[dy, :, 1], xp, f"plus{dy}")
        go(f"early-{dy}", y_out.at[1, dy, :, 0], r_minus.at[dy, :, 0], xm, f"minus{dy}")

    def add_far(dy):
        go.arrive_all(f"far+{dy}", r_far.at[dy, :, 0], xp)
        y_out[0, dy, :, 0] = (p_plus[dy, :, 0] + r_far[dy, :, 0].astype(F32)).astype(BF16)
        if dy == 1:
            go("late+1", y_out.at[0, 1, :, 0], r_plus.at[1, :, 0], xp, "plus1")
        else:
            for half in (0, 1):
                go(f"late+0{half}", y_out.at[0, 0, half, 0], r_plus.at[0, half, 0], xp)
        go.arrive_all(f"far-{dy}", r_far.at[dy, :, 1], xm)
        y_out[1, dy, :, 1] = (p_minus[dy, :, 1] + r_far[dy, :, 1].astype(F32)).astype(BF16)
        if dy == 1:
            go("late-1", y_out.at[1, 1, :, 1], r_minus.at[1, :, 1], xm, "minus1")
        else:
            for half in (0, 1):
                go(f"late-0{half}", y_out.at[1, 0, half, 1], r_minus.at[0, half, 1], xm)

    p_far[1] = project_two(1, 2)
    go.arrive("att2a")
    far_block(1, lower, 0)
    send_far(1, 0)
    go.arrive("att2b")
    far_block(1, upper, 1)
    send_far(1, 1)
    near_blocks(1)
    send_early(1)
    go.arrive("wz2+")
    go("wq1", wb.at[before, second], wb.at[before, second], yp)
    go.arrive("wz2-")
    go("wf2", wb.at[after, second], wb.at[after, second], zm)
    go.arrive_all("wy1", wb.at[opposite, first], yp)
    q1, q2 = pl.ds(0, SPLIT // 2), pl.ds(SPLIT // 2, SPLIT // 2)
    go("wp+a", wb.at[opposite, q1], wb.at[opposite, q1], zp)
    p_far[0] = project_two(0, 2)
    far_block(0, lower, 0)
    far_block(0, upper, 1)
    near_blocks(0)
    add_far(1)
    send_far(0, 0)
    send_far(0, 1)
    send_early(0)
    for dy in (1, 0):
        p_here[dy] = project_two(dy, 0) + project_last(dy, 0, whole)
    go.drain("n+2", "n-2", "f+1", "f-1", "f+2", "f-2", "s0", "o0", "s1", "o1", "att0", "att1")
    go.arrive_all("plus1", r_plus.at[1], xp)
    go.arrive_all("minus1", r_minus.at[1], xm)
    near = p_here[1] + (r_plus[1].astype(F32) + r_minus[1].astype(F32)).reshape(ROWS, OWN)
    y_in[0] = near.astype(BF16)
    go("rows", y_in.at[0], y_in.at[1], yq)
    chunk1, chunk2 = pl.ds(SPLIT, 64), pl.ds(SPLIT + 64, WIDE - SPLIT - 64)
    go("wq2a", wb.at[after, chunk1], wb.at[after, chunk1], yp, "wq2")
    rows1, rows2 = pl.ds(0, WIDE // 2), pl.ds(WIDE // 2, SPLIT - WIDE // 2)
    go.arrive("wz1+")
    go("wf1", wb.at[before, rows1], wb.at[before, rows1], zp, "wf")
    go.arrive("wz1-")
    go("wf3", wb.at[after, rows2], wb.at[after, rows2], zm, "wf")
    go("wp-a", wb.at[opposite, q2], wb.at[opposite, q2], zm)
    go("wp+b", wb.at[opposite, q2], wb.at[opposite, q2], zp)
    go("wp-b", wb.at[opposite, q1], wb.at[opposite, q1], zm)
    add_far(0)
    landed(6, stream_vm)
    own, other_chip = chip(0, 0), chip(1, 0)

    def block(j, half=slice(None), way=slice(None)):
        return xb.at[j, half, way, :, mine]

    def spread(dy, half):
        j = chip(dy, 0)
        go(f"x+{dy}{half}", block(j, half), block(j, half), xp)
        go(f"x-{dy}{half}", block(j, half), block(j, half), xm)

    def pass_core(dy):
        left, right = chip(dy, -1), chip(dy, 1)
        go(f"xc+{dy}", block(left), block(left), cp)
        go(f"xc-{dy}", block(right), block(right), cp)

    go.arrive_all("plus0", r_plus.at[0, :, 1], xp)
    go.arrive_all("minus0", r_minus.at[0, :, 0], xm)
    for half, rows in ((0, lower), (1, upper)):
        go.arrive(f"late+0{half}", f"late-0{half}")
        if half == 0:
            go.arrive("rows")
        here = p_here[0, rows, :] + (r_plus[0, half].astype(F32) + r_minus[0, half].astype(F32)).reshape(HALF, OWN)
        here = here + stream_vm[rows].astype(F32) + y_in[1, rows].astype(F32)
        residual = here.astype(BF16)
        xb[own, half, :, :, mine] = residual.reshape(2, QUARTER, OWN)
        residual_ref[rows] = residual
        spread(0, half)
        go(f"xy{half}", block(own, half), block(own, half), yq)

    def prepare(j, start=False):
        gain = gain_ref[:, pl.ds(pl.multiple_of(j * WIDE, 128), WIDE)]
        level = xb[j].reshape(ROWS, WIDE).astype(F32)
        xg[j] = (level * gain).astype(BF16)
        level = level * level
        sums = level[:, 0:128]
        for k in range(1, WIDE // 128):
            sums = sums + level[:, k * 128 : (k + 1) * 128]
        squares[...] = sums if start else squares[...] + sums

    def expand(j, start=False):
        product = jnp.dot(xg[j], wb[j], preferred_element_type=F32)
        total[...] = product if start else total[...] + product

    go("xc", block(own), block(own), cp)
    go("wq2b", wb.at[after, chunk2], wb.at[after, chunk2], yp, "wq2")
    go.arrive("wf2")
    go("wq3", wb.at[across, second], wb.at[across, second], yp)
    go.drain(*[f"early{sign}{dy}" for sign in "+-" for dy in (0, 1)])
    go.drain(*[f"far{sign}{dy}{half}" for sign in "+-" for dy in (0, 1) for half in (0, 1)])
    go.drain("s2a", "o2a", "s2b", "o2b", "att2a", "att2b", *[f"wy{i}" for i in range(0, 12, 2)])
    go.drain("wz2+", "wz2-", "wz1+", "wz1-", "late+1", "late-1")
    go.arrive("xy0")
    spread(1, 0)
    go.arrive("xc")
    prepare(own, start=True)
    go.arrive("xy1")
    spread(1, 1)
    go("xcy", block(other_chip), block(other_chip), cp)
    go.arrive("x+00", "x+01")
    go("xf+0", block(chip(0, -1), way=0), block(chip(0, -1), way=0), xp, "xf0")
    go.arrive("x-00", "x-01")
    go("xf-0", block(chip(0, 1), way=1), block(chip(0, 1), way=1), xm, "xf0")
    pass_core(0)
    go.arrive("wp+a")
    go("wpf+", wb.at[before_opposite, q1], wb.at[before_opposite, q1], zp, "wpf")
    go.arrive("wp-a")
    go("wpf-", wb.at[after_opposite, q2], wb.at[after_opposite, q2], zm, "wpf")
    go.arrive("xc+0")
    prepare(chip(0, -1))
    go.arrive("xc-0")
    prepare(chip(0, 1))
    go.arrive("xcy")
    prepare(other_chip)

    def pass_far(half):
        go.arrive(f"x+1{half}")
        go(f"xf+1{half}", block(chip(1, -1), half, 0), block(chip(1, -1), half, 0), xp, f"xf1{half}")
        go.arrive(f"x-1{half}")
        go(f"xf-1{half}", block(chip(1, 1), half, 1), block(chip(1, 1), half, 1), xm, f"xf1{half}")

    same = lax.rem(x + yh, 2)
    rest = 1 - same
    far_chip, last_chip = chip(0, 2), chip(1, 2)
    order = [
        chip(0, rest),
        jnp.where(same == 0, chip(0, 3), other_chip),
        chip(1, 1),
        chip(1, 3),
        far_chip,
    ]
    passed = order[0] == across_opposite
    turn = []
    for k in range(4):
        turn.append(jnp.where(passed, order[k + 1], order[k]))
        passed = passed | (order[k + 1] == across_opposite)
    turn.append(jnp.where(passed, across_opposite, order[4]))
    go.arrive_all("wf", wb.at[across, first], zp)
    expand(chip(0, same), start=True)
    pass_far(0)
    expand(jnp.where(same == 0, other_chip, chip(0, 3)))
    go.arrive_all("wy2", wb.at[opposite, second], yp)
    go.arrive("wq1", "wp+b", "wp-b")
    go.arrive_all("wq2", wb.at[after_opposite, second], yp)
    expand(turn[0])
    pass_far(1)
    pass_core(1)
    go.arrive("xc+1")
    prepare(chip(1, -1))
    go.arrive("xc-1")
    prepare(chip(1, 1))
    expand(turn[1])
    go.arrive_all("xf0", block(far_chip), xp)
    go("xcf0", block(far_chip), block(far_chip), cp)
    expand(turn[2])
    go.arrive("xcf0")
    prepare(far_chip)
    go.arrive_all("xf10", block(last_chip, 0), xp)
    go("xcf10", block(last_chip, 0), block(last_chip, 0), cp)
    expand(turn[3])
    go.arrive_all("xf11", block(last_chip, 1), xp)
    go("xcf11", block(last_chip, 1), block(last_chip, 1), cp)
    go.arrive("wq3")
    go.arrive_all("wpf", wb.at[across_opposite, first], zp)
    expand(turn[4])
    gain = gain_ref[:, pl.ds(pl.multiple_of(last_chip * WIDE, 128), WIDE)]
    for half, rows in ((0, lower), (1, upper)):
        go.arrive(f"xcf1{half}")
        level = xb[last_chip, half].reshape(HALF, WIDE).astype(F32)
        product = jnp.dot((level * gain).astype(BF16), wb[last_chip], preferred_element_type=F32)
        square = jnp.sum(level * level, axis=1, keepdims=True) + jnp.sum(squares[rows], axis=1, keepdims=True)
        inverse = lax.rsqrt(square * (1.0 / D) + 1e-6)
        expanded_ref[rows] = jax.nn.gelu((total[rows] + product) * inverse, approximate=True).astype(BF16)
    go.drain()
    assert go.used <= N_SEND and len(go.groups) <= N_RECV, (go.used, len(go.groups))


def body(queries, keys, values, stream, out_weight, norm_gain, up_weight):
    anywhere = pl.BlockSpec(memory_space=pl.ANY)
    vmem = pl.BlockSpec(memory_space=pltpu.VMEM)
    return pl.pallas_call(
        kernel,
        out_shape=(
            pltpu.VMEM((ROWS, OWN), BF16),
            pltpu.VMEM((ROWS, WIDE), BF16),
        ),
        in_specs=[anywhere, anywhere, anywhere, anywhere, anywhere, vmem, anywhere],
        out_specs=(vmem, vmem),
        scratch_shapes=[
            pltpu.VMEM((2, 3, ROWS, HD), BF16),
            pltpu.VMEM((3, 4, 2, ROWS, HD), BF16),
            pltpu.VMEM((3, ROWS, HD), BF16),
            pltpu.VMEM((3, 8, ROWS), F32),
            pltpu.VMEM((3, ROWS, HD), BF16),
            pltpu.VMEM((3, 8, ROWS), F32),
            pltpu.VMEM((2, 3, ROWS, HD), F32),
            pltpu.VMEM((2, 3, ROWS, HD), F32),
            pltpu.VMEM((3, ROWS, 2 * HD), BF16),
            pltpu.VMEM((8, 3, 2, HD, OWN), BF16),
            pltpu.VMEM((8, WIDE, WIDE), BF16),
            pltpu.VMEM((ROWS, OWN), BF16),
            pltpu.VMEM((2, ROWS, OWN), F32),
            pltpu.VMEM((2, 2, 2, QUARTER, OWN), BF16),
            pltpu.VMEM((2, 2, 2, QUARTER, OWN), F32),
            pltpu.VMEM((2, 2, 2, QUARTER, OWN), F32),
            pltpu.VMEM((2, ROWS, OWN), F32),
            pltpu.VMEM((2, 2, 2, QUARTER, OWN), BF16),
            pltpu.VMEM((2, 2, 2, QUARTER, OWN), BF16),
            pltpu.VMEM((2, 2, 2, QUARTER, OWN), BF16),
            pltpu.VMEM((2, 2, 2, 2, QUARTER, OWN), BF16),
            pltpu.VMEM((2, ROWS, OWN), BF16),
            pltpu.VMEM((8, 2, 2, QUARTER, WIDE), BF16),
            pltpu.VMEM((8, ROWS, WIDE), BF16),
            pltpu.VMEM((ROWS, WIDE), F32),
            pltpu.VMEM((ROWS, 128), F32),
            pltpu.SemaphoreType.DMA((N_SEND,)),
            pltpu.SemaphoreType.DMA((N_RECV,)),
            pltpu.SemaphoreType.DMA((N_LOCAL,)),
        ],
        compiler_params=pltpu.CompilerParams(
            collective_id=0, has_side_effects=True, vmem_limit_bytes=53 * 2**20
        ),
        cost_estimate=pl.CostEstimate(flops=10_500_000_000, bytes_accessed=12_000_000, transcendentals=6_300_000),
    )(queries, keys, values, stream, out_weight.reshape(3, HD, D), norm_gain.reshape(1, D), up_weight)


def solution(mesh):
    in_specs = (
        P("seq", "tensor"),
        P("seq", "tensor"),
        P("seq", "tensor"),
        P("seq", "tensor"),
        P("tensor", None),
        P(),
        P("seq", "tensor"),
    )
    out_specs = (P("seq", "tensor"), P("seq", "tensor"))
    return jax.shard_map(body, mesh=mesh, in_specs=in_specs, out_specs=out_specs, check_vma=False)
```

```python
import math

import jax
import jax.numpy as jnp
from jax import lax
from jax.experimental import pallas as pl
from jax.experimental.pallas import tpu as pltpu
from jax.sharding import PartitionSpec as P

D = 6144
HD = 128
EXPONENT = math.log2(math.e) / math.sqrt(HD)
MESH = pl.DeviceIdType.MESH
BF16 = jnp.bfloat16
F32 = jnp.float32

ROWS = 512
HALF = 256
QUARTER = 128
OWN = 384
WIDE = 768
SPLIT = 512


class Copies:
    def __init__(self, send, recv):
        self.send, self.recv = send, recv
        self.made, self.slots, self.groups = {}, {}, {}
        self.free, self.used = [], 0

    def __call__(self, name, src, dst, device, group=None):
        if not self.free:
            self.free.append(self.used)
            self.used += 1
        self.slots[name] = slot = self.free.pop()
        index = self.groups.setdefault(group or name, len(self.groups))
        self.made[name] = copy = pltpu.make_async_remote_copy(
            src_ref=src,
            dst_ref=dst,
            send_sem=self.send.at[slot],
            recv_sem=self.recv.at[index],
            device_id=device,
            device_id_type=MESH,
        )
        copy.start()

    def arrive(self, *names):
        for name in names:
            self.made[name].wait_recv()

    def arrive_all(self, group, ref, device):
        pltpu.make_async_remote_copy(
            src_ref=ref,
            dst_ref=ref,
            send_sem=self.send.at[0],
            recv_sem=self.recv.at[self.groups[group]],
            device_id=device,
            device_id_type=MESH,
        ).wait_recv()

    def drain(self, *names):
        for name in names or tuple(self.slots):
            self.made[name].wait_send()
            self.free.append(self.slots.pop(name))


N_SEND = 54
N_RECV = 75
N_LOCAL = 8


def kernel(
    q_ref, k_ref, v_ref, stream_ref, ow_ref, gain_ref, up_ref,
    residual_ref, expanded_ref,
    qb, kvb, o_out, st_out, o_in, st_in, o_part, st_part, att, owb, wb, stream_vm,
    p_far, p_out, p_plus, p_minus, p_here, r_far, r_plus, r_minus, y_out, y_in, xb, xg, total, squares,
    send, recv, local_sem,
):
    s = lax.axis_index("seq")
    t = lax.axis_index("tensor")
    z, yh = s // 2, lax.rem(s, 2)
    yl, x, c = t // 8, lax.rem(t // 2, 4), lax.rem(t, 2)

    def ring(a, d):
        return lax.rem(a + d + 4, 4)

    def token_block(dz, dy):
        return ring(z, dz) * 2 + (yh if dy == 0 else 1 - yh)

    def chip(dy, dx):
        return (yl if dy == 0 else 1 - yl) * 4 + ring(x, dx)

    zp, zm = (token_block(1, 0), t), (token_block(-1, 0), t)
    yp = (token_block(0, 1), t)
    xp, xm = (s, chip(0, 1) * 2 + c), (s, chip(0, -1) * 2 + c)
    yq = (s, chip(1, 0) * 2 + c)
    cp = (s, chip(0, 0) * 2 + 1 - c)
    partners = (zp, zm, yp, xp, xm, yq, cp)

    barrier = pltpu.get_barrier_semaphore()
    for device in partners:
        pl.semaphore_signal(barrier, inc=1, device_id=device, device_id_type=MESH)

    def local(index, *pairs):
        for src, dst in pairs:
            pltpu.make_async_copy(src, dst, local_sem.at[index]).start()

    def landed(index, ref):
        pltpu.make_async_copy(ref, ref, local_sem.at[index]).wait()

    def head_columns(h):
        return pl.ds(h * HD, HD)

    for h in range(3):
        local(
            h,
            (k_ref.at[:, head_columns(h)], kvb.at[h, 0, 0]),
            (v_ref.at[:, head_columns(h)], kvb.at[h, 0, 1]),
        )
    local(3, *[(q_ref.at[:, head_columns(h)], qb.at[0, h]) for h in range(3)])
    local(4, (up_ref, wb.at[s]))
    mine = pl.ds(pl.multiple_of(c * OWN, 128), OWN)

    def feature_block(j, core):
        return pl.ds(pl.multiple_of((2 * j + core) * OWN, 128), OWN)

    local(5, *[(ow_ref.at[:, :, feature_block(j, c)], owb.at[j, :, c]) for j in range(8)])
    local(6, (stream_ref, stream_vm))

    def greeted():
        pl.semaphore_wait(barrier, len(partners))

    greeted()
    go = Copies(send, recv)

    lower, upper = pl.ds(0, HALF), pl.ds(HALF, HALF)

    def near(h):
        go(f"n+{h}", kvb.at[h, 0], kvb.at[h, 1], zp)
        go(f"n-{h}", kvb.at[h, 0], kvb.at[h, 2], zm)

    def far(h):
        go.arrive(f"n+{h}")
        go(f"f+{h}", kvb.at[h, 1, :, lower], kvb.at[h, 3, :, lower], zp, f"f{h}")
        go.arrive(f"n-{h}")
        go(f"f-{h}", kvb.at[h, 2, :, upper], kvb.at[h, 3, :, upper], zm, f"f{h}")

    def scores_of(which, h, rows, slots):
        keys = kvb[h, slots, 0].reshape(-1, HD)
        return lax.dot_general(
            qb[which, h, rows, :], keys, (((1,), (1,)), ((), ())), preferred_element_type=F32
        )

    lane = lax.broadcasted_iota(jnp.int32, (HALF, HD), 1)

    def attend_near(which, h):
        def tile(i, carry):
            rows = pl.ds(pl.multiple_of(i * HALF, HALF), HALF)
            slots = slice(0, 3)
            scores = scores_of(which, h, rows, slots)
            top = jnp.max(scores, axis=1, keepdims=True)
            weights = jnp.exp2((scores - top) * EXPONENT)
            bottom = jnp.sum(weights, axis=1, keepdims=True)
            o_part[which, h, rows, :] = jnp.dot(
                weights.astype(BF16), kvb[h, slots, 1].reshape(-1, HD), preferred_element_type=F32
            )
            st_part[which, h, rows, :] = jnp.where(lane == 0, top, bottom)
            return carry

        lax.fori_loop(0, 2, tile, 0)

    def attend_far(which, h, halves=None):
        def tile(i, carry):
            rows = pl.ds(i * HALF if isinstance(i, int) else pl.multiple_of(i * HALF, HALF), HALF)
            slots = slice(3, 4)
            scores = scores_of(which, h, rows, slots)
            stats = st_part[which, h, rows, :]
            top_near, bottom_near = stats[:, 0:1], stats[:, 1:2]
            top = jnp.maximum(top_near, jnp.max(scores, axis=1, keepdims=True))
            weights = jnp.exp2((scores - top) * EXPONENT)
            decay = jnp.exp2((top_near - top) * EXPONENT)
            bottom = bottom_near * decay + jnp.sum(weights, axis=1, keepdims=True)
            out = jnp.dot(weights.astype(BF16), kvb[h, slots, 1].reshape(-1, HD), preferred_element_type=F32)
            out = (o_part[which, h, rows, :] * decay + out) / bottom
            both = jnp.where(lane == 0, top, bottom)
            if which == 1:
                o_out[h, rows, :] = out.astype(BF16)
                st_out[h, :, rows] = both.T[:8]
            else:
                o_part[0, h, rows, :] = out
                st_part[0, h, rows, :] = both
            return carry

        if halves is None:
            lax.fori_loop(0, 2, tile, 0)
        else:
            tile(halves, 0)

    def give_back(h, part="", rows=slice(None)):
        go(f"s{h}{part}", st_out.at[h, :, rows], st_in.at[h, :, rows], yp)
        go(f"o{h}{part}", o_out.at[h, rows], o_in.at[h, rows], yp)

    landed(0, kvb.at[0, 0])
    near(0)
    landed(1, kvb.at[1, 0])
    near(1)
    landed(3, qb.at[0])
    for h in range(3):
        go(f"q{h}", qb.at[0, h], qb.at[1, h], yp)
    for j in range(8):
        go(f"ow{j}", ow_ref.at[:, :, feature_block(j, 1 - c)], owb.at[j, :, c], cp, "ow")
    landed(2, kvb.at[2, 0])
    landed(4, wb.at[s])
    first, second = pl.ds(0, SPLIT), pl.ds(SPLIT, WIDE - SPLIT)
    own_rows = token_block(0, 0)

    def cross(i, n=2):
        rows = pl.ds(i * 64, n * 64)
        go(f"wy{i}", wb.at[own_rows, rows], wb.at[own_rows, rows], yp, "wy1" if i < SPLIT // 64 else "wy2")

    cross(0)
    cross(2)
    cross(4, 1)
    far(0)
    near(2)
    go.arrive("q0")
    attend_near(1, 0)
    attend_near(0, 0)
    far(1)
    go.arrive("q1")
    attend_near(1, 1)
    attend_near(0, 1)
    go.arrive_all("f0", kvb.at[0, 3], zp)
    attend_far(1, 0)
    give_back(0)
    cross(5)
    cross(7, 1)
    attend_far(0, 0)
    far(2)
    go.arrive("q2")
    attend_near(1, 2)
    attend_near(0, 2)
    go("wz2+", wb.at[own_rows, second], wb.at[own_rows, second], zp)
    go("wz2-", wb.at[own_rows, second], wb.at[own_rows, second], zm)
    go("wz1+", wb.at[own_rows, first], wb.at[own_rows, first], zp)
    go("wz1-", wb.at[own_rows, first], wb.at[own_rows, first], zm)
    go.arrive_all("f1", kvb.at[1, 3], zp)
    attend_far(1, 1)
    give_back(1)
    go.arrive_all("f2", kvb.at[2, 3], zp)
    attend_far(1, 2, 0)
    give_back(2, "a", lower)
    attend_far(1, 2, 1)
    give_back(2, "b", upper)
    attend_far(0, 1)
    attend_far(0, 2)

    def merge(h, rows):
        theirs = jnp.concatenate([st_in[h, :, rows]] * 16, axis=0).T
        ours = st_part[0, h, rows, :]
        top1, sum1 = ours[:, 0:1], ours[:, 1:2]
        top2, sum2 = theirs[:, 0:1], theirs[:, 1:2]
        top = jnp.maximum(top1, top2)
        w1 = sum1 * jnp.exp2((top1 - top) * EXPONENT)
        w2 = sum2 * jnp.exp2((top2 - top) * EXPONENT)
        scale = 1.0 / (w1 + w2)
        merged = (w1 * scale) * o_part[0, h, rows, :] + (w2 * scale) * o_in[h, rows, :].astype(F32)
        att[h, rows, own_half] = merged.astype(BF16)

    own_half = pl.ds(pl.multiple_of(c * HD, HD), HD)
    whole = pl.ds(0, ROWS)
    for h in range(2):
        go.arrive(f"s{h}", f"o{h}")
        merge(h, whole)
        go(f"att{h}", att.at[h, :, own_half], att.at[h, :, own_half], cp, "att")
    go.drain(*[f"{kind}{h}" for kind in ("n+", "n-") for h in range(2)], "f+0", "f-0", "q0", "q1", "q2")
    go.drain(*[f"ow{j}" for j in range(8)])
    for part, rows in (("a", lower), ("b", upper)):
        go.arrive(f"s2{part}", f"o2{part}")
        merge(2, rows)
        go(f"att2{part}", att.at[2, rows, own_half], att.at[2, rows, own_half], cp)
    cross(8)
    cross(10)
    landed(5, owb.at[:, :, c])
    go.arrive_all("ow", owb.at[:, :, 1 - c], cp)
    go.arrive_all("att", att.at[0:2, :, own_half], cp)

    def project_two(dy, dx):
        return jnp.dot(
            jnp.concatenate([att[0], att[1]], axis=1),
            owb[chip(dy, dx), 0:2].reshape(4 * HD, OWN),
            preferred_element_type=F32,
        )

    def project_last(dy, dx, rows):
        return jnp.dot(
            att[2, rows, :], owb[chip(dy, dx), 2].reshape(2 * HD, OWN), preferred_element_type=F32
        )

    before, after, across = token_block(-1, 0), token_block(1, 0), token_block(2, 0)
    opposite = token_block(0, 1)
    before_opposite, after_opposite, across_opposite = token_block(-1, 1), token_block(1, 1), token_block(2, 1)

    def quarters(a):
        return a.reshape(2, 2, QUARTER, OWN)

    def send_far(dy, half):
        go(f"far+{dy}{half}", p_out.at[dy, half, 0], r_far.at[dy, half, 0], xp, f"far+{dy}")
        go(f"far-{dy}{half}", p_out.at[dy, half, 1], r_far.at[dy, half, 1], xm, f"far-{dy}")

    def far_block(dy, rows, half):
        out = p_far[dy, rows, :] + project_last(dy, 2, rows)
        p_out[dy, half] = out.astype(BF16).reshape(2, QUARTER, OWN)

    def near_blocks(dy):
        p_plus[dy] = quarters(project_two(dy, 1) + project_last(dy, 1, whole))
        y_out[0, dy, :, 1] = p_plus[dy, :, 1].astype(BF16)
        p_minus[dy] = quarters(project_two(dy, -1) + project_last(dy, -1, whole))
        y_out[1, dy, :, 0] = p_minus[dy, :, 0].astype(BF16)

    def send_early(dy):
        go(f"early+{dy}", y_out.at[0, dy, :, 1], r_plus.at[dy, :, 1], xp, f"plus{dy}")
        go(f"early-{dy}", y_out.at[1, dy, :, 0], r_minus.at[dy, :, 0], xm, f"minus{dy}")

    def add_far(dy):
        go.arrive_all(f"far+{dy}", r_far.at[dy, :, 0], xp)
        y_out[0, dy, :, 0] = (p_plus[dy, :, 0] + r_far[dy, :, 0].astype(F32)).astype(BF16)
        if dy == 1:
            go("late+1", y_out.at[0, 1, :, 0], r_plus.at[1, :, 0], xp, "plus1")
        else:
            for half in (0, 1):
                go(f"late+0{half}", y_out.at[0, 0, half, 0], r_plus.at[0, half, 0], xp)
        go.arrive_all(f"far-{dy}", r_far.at[dy, :, 1], xm)
        y_out[1, dy, :, 1] = (p_minus[dy, :, 1] + r_far[dy, :, 1].astype(F32)).astype(BF16)
        if dy == 1:
            go("late-1", y_out.at[1, 1, :, 1], r_minus.at[1, :, 1], xm, "minus1")
        else:
            for half in (0, 1):
                go(f"late-0{half}", y_out.at[1, 0, half, 1], r_minus.at[0, half, 1], xm)

    p_far[1] = project_two(1, 2)
    go.arrive("att2a")
    far_block(1, lower, 0)
    send_far(1, 0)
    go.arrive("att2b")
    far_block(1, upper, 1)
    send_far(1, 1)
    near_blocks(1)
    send_early(1)
    go.arrive("wz2+")
    go("wq1", wb.at[before, second], wb.at[before, second], yp)
    go.arrive("wz2-")
    go("wf2", wb.at[after, second], wb.at[after, second], zm)
    go.arrive_all("wy1", wb.at[opposite, first], yp)
    q1, q2 = pl.ds(0, SPLIT // 2), pl.ds(SPLIT // 2, SPLIT // 2)
    go("wp+a", wb.at[opposite, q1], wb.at[opposite, q1], zp)
    p_far[0] = project_two(0, 2)
    far_block(0, lower, 0)
    far_block(0, upper, 1)
    near_blocks(0)
    add_far(1)
    send_far(0, 0)
    send_far(0, 1)
    send_early(0)
    for dy in (1, 0):
        p_here[dy] = project_two(dy, 0) + project_last(dy, 0, whole)
    go.drain("n+2", "n-2", "f+1", "f-1", "f+2", "f-2", "s0", "o0", "s1", "o1", "att0", "att1")
    go.arrive_all("plus1", r_plus.at[1], xp)
    go.arrive_all("minus1", r_minus.at[1], xm)
    near = p_here[1] + (r_plus[1].astype(F32) + r_minus[1].astype(F32)).reshape(ROWS, OWN)
    y_in[0] = near.astype(BF16)
    go("rows", y_in.at[0], y_in.at[1], yq)
    chunk1, chunk2 = pl.ds(SPLIT, 64), pl.ds(SPLIT + 64, WIDE - SPLIT - 64)
    go("wq2a", wb.at[after, chunk1], wb.at[after, chunk1], yp, "wq2")
    rows1, rows2 = pl.ds(0, WIDE // 2), pl.ds(WIDE // 2, SPLIT - WIDE // 2)
    go.arrive("wz1+")
    go("wf1", wb.at[before, rows1], wb.at[before, rows1], zp, "wf")
    go.arrive("wz1-")
    go("wf3", wb.at[after, rows2], wb.at[after, rows2], zm, "wf")
    go("wp-a", wb.at[opposite, q2], wb.at[opposite, q2], zm)
    go("wp+b", wb.at[opposite, q2], wb.at[opposite, q2], zp)
    go("wp-b", wb.at[opposite, q1], wb.at[opposite, q1], zm)
    add_far(0)
    landed(6, stream_vm)
    own, other_chip = chip(0, 0), chip(1, 0)

    def block(j, half=slice(None), way=slice(None)):
        return xb.at[j, half, way, :, mine]

    def spread(dy, half):
        j = chip(dy, 0)
        go(f"x+{dy}{half}", block(j, half), block(j, half), xp)
        go(f"x-{dy}{half}", block(j, half), block(j, half), xm)

    def pass_core(dy):
        left, right = chip(dy, -1), chip(dy, 1)
        go(f"xc+{dy}", block(left), block(left), cp)
        go(f"xc-{dy}", block(right), block(right), cp)

    go.arrive_all("plus0", r_plus.at[0, :, 1], xp)
    go.arrive_all("minus0", r_minus.at[0, :, 0], xm)
    for half, rows in ((0, lower), (1, upper)):
        go.arrive(f"late+0{half}", f"late-0{half}")
        if half == 0:
            go.arrive("rows")
        here = p_here[0, rows, :] + (r_plus[0, half].astype(F32) + r_minus[0, half].astype(F32)).reshape(HALF, OWN)
        here = here + stream_vm[rows].astype(F32) + y_in[1, rows].astype(F32)
        residual = here.astype(BF16)
        xb[own, half, :, :, mine] = residual.reshape(2, QUARTER, OWN)
        residual_ref[rows] = residual
        spread(0, half)
        go(f"xy{half}", block(own, half), block(own, half), yq)

    def prepare(j, start=False):
        gain = gain_ref[:, pl.ds(pl.multiple_of(j * WIDE, 128), WIDE)]
        level = xb[j].reshape(ROWS, WIDE).astype(F32)
        xg[j] = (level * gain).astype(BF16)
        level = level * level
        sums = level[:, 0:128]
        for k in range(1, WIDE // 128):
            sums = sums + level[:, k * 128 : (k + 1) * 128]
        squares[...] = sums if start else squares[...] + sums

    def expand(j, start=False):
        product = jnp.dot(xg[j], wb[j], preferred_element_type=F32)
        total[...] = product if start else total[...] + product

    go("xc", block(own), block(own), cp)
    go("wq2b", wb.at[after, chunk2], wb.at[after, chunk2], yp, "wq2")
    go.arrive("wf2")
    go("wq3", wb.at[across, second], wb.at[across, second], yp)
    go.drain(*[f"early{sign}{dy}" for sign in "+-" for dy in (0, 1)])
    go.drain(*[f"far{sign}{dy}{half}" for sign in "+-" for dy in (0, 1) for half in (0, 1)])
    go.drain("s2a", "o2a", "s2b", "o2b", "att2a", "att2b", *[f"wy{i}" for i in (0, 2, 4, 5, 7, 8, 10)])
    go.drain("wz2+", "wz2-", "wz1+", "wz1-", "late+1", "late-1")
    go.arrive("xy0")
    spread(1, 0)
    go.arrive("xc")
    prepare(own, start=True)
    go.arrive("xy1")
    spread(1, 1)
    go("xcy", block(other_chip), block(other_chip), cp)
    go.arrive("x+00", "x+01")
    go("xf+0", block(chip(0, -1), way=0), block(chip(0, -1), way=0), xp, "xf0")
    go.arrive("x-00", "x-01")
    go("xf-0", block(chip(0, 1), way=1), block(chip(0, 1), way=1), xm, "xf0")
    pass_core(0)
    go.arrive("wp+a")
    go("wpf+", wb.at[before_opposite, q1], wb.at[before_opposite, q1], zp, "wpf")
    go.arrive("wp-a")
    go("wpf-", wb.at[after_opposite, q2], wb.at[after_opposite, q2], zm, "wpf")
    go.arrive("xc+0")
    prepare(chip(0, -1))
    go.arrive("xc-0")
    prepare(chip(0, 1))
    go.arrive("xcy")
    prepare(other_chip)

    def pass_far(half):
        go.arrive(f"x+1{half}")
        go(f"xf+1{half}", block(chip(1, -1), half, 0), block(chip(1, -1), half, 0), xp, f"xf1{half}")
        go.arrive(f"x-1{half}")
        go(f"xf-1{half}", block(chip(1, 1), half, 1), block(chip(1, 1), half, 1), xm, f"xf1{half}")

    same = lax.rem(x + yh, 2)
    rest = 1 - same
    far_chip, last_chip = chip(0, 2), chip(1, 2)
    order = [
        chip(0, rest),
        jnp.where(same == 0, chip(0, 3), other_chip),
        chip(1, 1),
        chip(1, 3),
        far_chip,
    ]
    passed = order[0] == across_opposite
    turn = []
    for k in range(4):
        turn.append(jnp.where(passed, order[k + 1], order[k]))
        passed = passed | (order[k + 1] == across_opposite)
    turn.append(jnp.where(passed, across_opposite, order[4]))
    go.arrive_all("wf", wb.at[across, first], zp)
    expand(chip(0, same), start=True)
    pass_far(0)
    expand(jnp.where(same == 0, other_chip, chip(0, 3)))
    go.arrive_all("wy2", wb.at[opposite, second], yp)
    go.arrive("wq1", "wp+b", "wp-b")
    go.arrive_all("wq2", wb.at[after_opposite, second], yp)
    expand(turn[0])
    pass_far(1)
    pass_core(1)
    go.arrive("xc+1")
    prepare(chip(1, -1))
    go.arrive("xc-1")
    prepare(chip(1, 1))
    expand(turn[1])
    go.arrive_all("xf0", block(far_chip), xp)
    go("xcf0", block(far_chip), block(far_chip), cp)
    expand(turn[2])
    go.arrive("xcf0")
    prepare(far_chip)
    go.arrive_all("xf10", block(last_chip, 0), xp)
    go("xcf10", block(last_chip, 0), block(last_chip, 0), cp)
    expand(turn[3])
    go.arrive_all("xf11", block(last_chip, 1), xp)
    go("xcf11", block(last_chip, 1), block(last_chip, 1), cp)
    go.arrive("wq3")
    go.arrive_all("wpf", wb.at[across_opposite, first], zp)
    expand(turn[4])
    gain = gain_ref[:, pl.ds(pl.multiple_of(last_chip * WIDE, 128), WIDE)]
    for half, rows in ((0, lower), (1, upper)):
        go.arrive(f"xcf1{half}")
        level = xb[last_chip, half].reshape(HALF, WIDE).astype(F32)
        product = jnp.dot((level * gain).astype(BF16), wb[last_chip], preferred_element_type=F32)
        square = jnp.sum(level * level, axis=1, keepdims=True) + jnp.sum(squares[rows], axis=1, keepdims=True)
        inverse = lax.rsqrt(square * (1.0 / D) + 1e-6)
        expanded_ref[rows] = jax.nn.gelu((total[rows] + product) * inverse, approximate=True).astype(BF16)
    go.drain()
    assert go.used <= N_SEND and len(go.groups) <= N_RECV, (go.used, len(go.groups))


def body(queries, keys, values, stream, out_weight, norm_gain, up_weight):
    anywhere = pl.BlockSpec(memory_space=pl.ANY)
    vmem = pl.BlockSpec(memory_space=pltpu.VMEM)
    return pl.pallas_call(
        kernel,
        out_shape=(
            pltpu.VMEM((ROWS, OWN), BF16),
            pltpu.VMEM((ROWS, WIDE), BF16),
        ),
        in_specs=[anywhere, anywhere, anywhere, anywhere, anywhere, vmem, anywhere],
        out_specs=(vmem, vmem),
        scratch_shapes=[
            pltpu.VMEM((2, 3, ROWS, HD), BF16),
            pltpu.VMEM((3, 4, 2, ROWS, HD), BF16),
            pltpu.VMEM((3, ROWS, HD), BF16),
            pltpu.VMEM((3, 8, ROWS), F32),
            pltpu.VMEM((3, ROWS, HD), BF16),
            pltpu.VMEM((3, 8, ROWS), F32),
            pltpu.VMEM((2, 3, ROWS, HD), F32),
            pltpu.VMEM((2, 3, ROWS, HD), F32),
            pltpu.VMEM((3, ROWS, 2 * HD), BF16),
            pltpu.VMEM((8, 3, 2, HD, OWN), BF16),
            pltpu.VMEM((8, WIDE, WIDE), BF16),
            pltpu.VMEM((ROWS, OWN), BF16),
            pltpu.VMEM((2, ROWS, OWN), F32),
            pltpu.VMEM((2, 2, 2, QUARTER, OWN), BF16),
            pltpu.VMEM((2, 2, 2, QUARTER, OWN), F32),
            pltpu.VMEM((2, 2, 2, QUARTER, OWN), F32),
            pltpu.VMEM((2, ROWS, OWN), F32),
            pltpu.VMEM((2, 2, 2, QUARTER, OWN), BF16),
            pltpu.VMEM((2, 2, 2, QUARTER, OWN), BF16),
            pltpu.VMEM((2, 2, 2, QUARTER, OWN), BF16),
            pltpu.VMEM((2, 2, 2, 2, QUARTER, OWN), BF16),
            pltpu.VMEM((2, ROWS, OWN), BF16),
            pltpu.VMEM((8, 2, 2, QUARTER, WIDE), BF16),
            pltpu.VMEM((8, ROWS, WIDE), BF16),
            pltpu.VMEM((ROWS, WIDE), F32),
            pltpu.VMEM((ROWS, 128), F32),
            pltpu.SemaphoreType.DMA((N_SEND,)),
            pltpu.SemaphoreType.DMA((N_RECV,)),
            pltpu.SemaphoreType.DMA((N_LOCAL,)),
        ],
        compiler_params=pltpu.CompilerParams(
            collective_id=0, has_side_effects=True, vmem_limit_bytes=53 * 2**20
        ),
        cost_estimate=pl.CostEstimate(flops=10_500_000_000, bytes_accessed=12_000_000, transcendentals=6_300_000),
    )(queries, keys, values, stream, out_weight.reshape(3, HD, D), norm_gain.reshape(1, D), up_weight)


def solution(mesh):
    in_specs = (
        P("seq", "tensor"),
        P("seq", "tensor"),
        P("seq", "tensor"),
        P("seq", "tensor"),
        P("tensor", None),
        P(),
        P("seq", "tensor"),
    )
    out_specs = (P("seq", "tensor"), P("seq", "tensor"))
    return jax.shard_map(body, mesh=mesh, in_specs=in_specs, out_specs=out_specs, check_vma=False)
```

```python
import math

import jax
import jax.numpy as jnp
from jax import lax
from jax.experimental import pallas as pl
from jax.experimental.pallas import tpu as pltpu
from jax.sharding import PartitionSpec as P

D = 6144
HD = 128
EXPONENT = math.log2(math.e) / math.sqrt(HD)
MESH = pl.DeviceIdType.MESH
BF16 = jnp.bfloat16
F32 = jnp.float32

ROWS = 512
HALF = 256
QUARTER = 128
OWN = 384
WIDE = 768
SPLIT = 512


class Copies:
    def __init__(self, send, recv):
        self.send, self.recv = send, recv
        self.made, self.slots, self.groups = {}, {}, {}
        self.free, self.used = [], 0

    def __call__(self, name, src, dst, device, group=None):
        if not self.free:
            self.free.append(self.used)
            self.used += 1
        self.slots[name] = slot = self.free.pop()
        index = self.groups.setdefault(group or name, len(self.groups))
        self.made[name] = copy = pltpu.make_async_remote_copy(
            src_ref=src,
            dst_ref=dst,
            send_sem=self.send.at[slot],
            recv_sem=self.recv.at[index],
            device_id=device,
            device_id_type=MESH,
        )
        copy.start()

    def arrive(self, *names):
        for name in names:
            self.made[name].wait_recv()

    def arrive_all(self, group, ref, device):
        pltpu.make_async_remote_copy(
            src_ref=ref,
            dst_ref=ref,
            send_sem=self.send.at[0],
            recv_sem=self.recv.at[self.groups[group]],
            device_id=device,
            device_id_type=MESH,
        ).wait_recv()

    def drain(self, *names):
        for name in names or tuple(self.slots):
            self.made[name].wait_send()
            self.free.append(self.slots.pop(name))


N_SEND = 54
EARLY = 384
AHEAD = 160
N_RECV = 75
N_LOCAL = 8


def kernel(
    q_ref, k_ref, v_ref, stream_ref, ow_ref, gain_ref, up_ref,
    residual_ref, expanded_ref,
    qb, kvb, o_out, st_out, o_in, st_in, o_part, st_part, att, owb, wb, stream_vm,
    p_far, p_out, p_plus, p_minus, p_here, r_far, r_plus, r_minus, y_out, y_in, xb, xg, total, squares,
    send, recv, local_sem,
):
    s = lax.axis_index("seq")
    t = lax.axis_index("tensor")
    z, yh = s // 2, lax.rem(s, 2)
    yl, x, c = t // 8, lax.rem(t // 2, 4), lax.rem(t, 2)

    def ring(a, d):
        return lax.rem(a + d + 4, 4)

    def token_block(dz, dy):
        return ring(z, dz) * 2 + (yh if dy == 0 else 1 - yh)

    def chip(dy, dx):
        return (yl if dy == 0 else 1 - yl) * 4 + ring(x, dx)

    zp, zm = (token_block(1, 0), t), (token_block(-1, 0), t)
    yp = (token_block(0, 1), t)
    xp, xm = (s, chip(0, 1) * 2 + c), (s, chip(0, -1) * 2 + c)
    yq = (s, chip(1, 0) * 2 + c)
    cp = (s, chip(0, 0) * 2 + 1 - c)
    partners = (zp, zm, yp, xp, xm, yq, cp)

    barrier = pltpu.get_barrier_semaphore()
    for device in partners:
        pl.semaphore_signal(barrier, inc=1, device_id=device, device_id_type=MESH)

    def local(index, *pairs):
        for src, dst in pairs:
            pltpu.make_async_copy(src, dst, local_sem.at[index]).start()

    def landed(index, ref):
        pltpu.make_async_copy(ref, ref, local_sem.at[index]).wait()

    def head_columns(h):
        return pl.ds(h * HD, HD)

    for h in range(3):
        local(
            h,
            (k_ref.at[:, head_columns(h)], kvb.at[h, 0, 0]),
            (v_ref.at[:, head_columns(h)], kvb.at[h, 0, 1]),
        )
    local(3, *[(q_ref.at[:, head_columns(h)], qb.at[0, h]) for h in range(3)])
    local(4, (up_ref, wb.at[s]))
    mine = pl.ds(pl.multiple_of(c * OWN, 128), OWN)

    def feature_block(j, core):
        return pl.ds(pl.multiple_of((2 * j + core) * OWN, 128), OWN)

    local(5, *[(ow_ref.at[:, :, feature_block(j, c)], owb.at[j, :, c]) for j in range(8)])
    local(6, (stream_ref, stream_vm))

    def greeted():
        pl.semaphore_wait(barrier, len(partners))

    greeted()
    go = Copies(send, recv)

    lower, upper = pl.ds(0, HALF), pl.ds(HALF, HALF)

    def near(h):
        go(f"n+{h}", kvb.at[h, 0], kvb.at[h, 1], zp)
        go(f"n-{h}", kvb.at[h, 0], kvb.at[h, 2], zm)

    def far(h):
        go.arrive(f"n+{h}")
        go(f"f+{h}", kvb.at[h, 1, :, lower], kvb.at[h, 3, :, lower], zp, f"f{h}")
        go.arrive(f"n-{h}")
        go(f"f-{h}", kvb.at[h, 2, :, upper], kvb.at[h, 3, :, upper], zm, f"f{h}")

    def scores_of(which, h, rows, slots):
        keys = kvb[h, slots, 0].reshape(-1, HD)
        return lax.dot_general(
            qb[which, h, rows, :], keys, (((1,), (1,)), ((), ())), preferred_element_type=F32
        )

    lane = lax.broadcasted_iota(jnp.int32, (HALF, HD), 1)

    def attend_near(which, h):
        def tile(i, carry):
            rows = pl.ds(pl.multiple_of(i * HALF, HALF), HALF)
            slots = slice(0, 3)
            scores = scores_of(which, h, rows, slots)
            top = jnp.max(scores, axis=1, keepdims=True)
            weights = jnp.exp2((scores - top) * EXPONENT)
            bottom = jnp.sum(weights, axis=1, keepdims=True)
            o_part[which, h, rows, :] = jnp.dot(
                weights.astype(BF16), kvb[h, slots, 1].reshape(-1, HD), preferred_element_type=F32
            )
            st_part[which, h, rows, :] = jnp.where(lane == 0, top, bottom)
            return carry

        lax.fori_loop(0, 2, tile, 0)

    def attend_far(which, h, halves=None):
        def tile(i, carry):
            rows = pl.ds(i * HALF if isinstance(i, int) else pl.multiple_of(i * HALF, HALF), HALF)
            slots = slice(3, 4)
            scores = scores_of(which, h, rows, slots)
            stats = st_part[which, h, rows, :]
            top_near, bottom_near = stats[:, 0:1], stats[:, 1:2]
            top = jnp.maximum(top_near, jnp.max(scores, axis=1, keepdims=True))
            weights = jnp.exp2((scores - top) * EXPONENT)
            decay = jnp.exp2((top_near - top) * EXPONENT)
            bottom = bottom_near * decay + jnp.sum(weights, axis=1, keepdims=True)
            out = jnp.dot(weights.astype(BF16), kvb[h, slots, 1].reshape(-1, HD), preferred_element_type=F32)
            out = (o_part[which, h, rows, :] * decay + out) / bottom
            both = jnp.where(lane == 0, top, bottom)
            if which == 1:
                o_out[h, rows, :] = out.astype(BF16)
                st_out[h, :, rows] = both.T[:8]
            else:
                o_part[0, h, rows, :] = out
                st_part[0, h, rows, :] = both
            return carry

        if halves is None:
            lax.fori_loop(0, 2, tile, 0)
        else:
            tile(halves, 0)

    def give_back(h, part="", rows=slice(None)):
        go(f"s{h}{part}", st_out.at[h, :, rows], st_in.at[h, :, rows], yp)
        go(f"o{h}{part}", o_out.at[h, rows], o_in.at[h, rows], yp)

    landed(0, kvb.at[0, 0])
    near(0)
    landed(1, kvb.at[1, 0])
    near(1)
    landed(3, qb.at[0])
    for h in range(3):
        go(f"q{h}", qb.at[0, h], qb.at[1, h], yp)
    for j in range(8):
        go(f"ow{j}", ow_ref.at[:, :, feature_block(j, 1 - c)], owb.at[j, :, c], cp, "ow")
    landed(2, kvb.at[2, 0])
    landed(4, wb.at[s])
    first, second = pl.ds(0, SPLIT), pl.ds(SPLIT, WIDE - SPLIT)
    own_rows = token_block(0, 0)

    def cross(start, stop):
        rows = pl.ds(start, stop - start)
        go(f"wy{start}", wb.at[own_rows, rows], wb.at[own_rows, rows], yp, "wy1" if start < SPLIT else "wy2")

    cross(0, 128)
    cross(128, 256)
    far(0)
    near(2)
    go.arrive("q0")
    attend_near(1, 0)
    attend_near(0, 0)
    far(1)
    go.arrive("q1")
    attend_near(1, 1)
    attend_near(0, 1)
    go.arrive_all("f0", kvb.at[0, 3], zp)
    attend_far(1, 0)
    give_back(0)
    cross(256, EARLY)
    attend_far(0, 0)
    far(2)
    go.arrive("q2")
    attend_near(1, 2)
    attend_near(0, 2)
    go("wz2+", wb.at[own_rows, second], wb.at[own_rows, second], zp)
    go("wz2-", wb.at[own_rows, second], wb.at[own_rows, second], zm)
    go("wz1+", wb.at[own_rows, first], wb.at[own_rows, first], zp)
    go("wz1-", wb.at[own_rows, first], wb.at[own_rows, first], zm)
    go.arrive_all("f1", kvb.at[1, 3], zp)
    attend_far(1, 1)
    give_back(1)
    go.arrive_all("f2", kvb.at[2, 3], zp)
    attend_far(1, 2, 0)
    give_back(2, "a", lower)
    attend_far(1, 2, 1)
    give_back(2, "b", upper)
    attend_far(0, 1)
    attend_far(0, 2)

    def merge(h, rows):
        theirs = jnp.concatenate([st_in[h, :, rows]] * 16, axis=0).T
        ours = st_part[0, h, rows, :]
        top1, sum1 = ours[:, 0:1], ours[:, 1:2]
        top2, sum2 = theirs[:, 0:1], theirs[:, 1:2]
        top = jnp.maximum(top1, top2)
        w1 = sum1 * jnp.exp2((top1 - top) * EXPONENT)
        w2 = sum2 * jnp.exp2((top2 - top) * EXPONENT)
        scale = 1.0 / (w1 + w2)
        merged = (w1 * scale) * o_part[0, h, rows, :] + (w2 * scale) * o_in[h, rows, :].astype(F32)
        att[h, rows, own_half] = merged.astype(BF16)

    own_half = pl.ds(pl.multiple_of(c * HD, HD), HD)
    whole = pl.ds(0, ROWS)
    for h in range(2):
        go.arrive(f"s{h}", f"o{h}")
        merge(h, whole)
        go(f"att{h}", att.at[h, :, own_half], att.at[h, :, own_half], cp, "att")
    go.drain(*[f"{kind}{h}" for kind in ("n+", "n-") for h in range(2)], "f+0", "f-0", "q0", "q1", "q2")
    go.drain(*[f"ow{j}" for j in range(8)])
    for part, rows in (("a", lower), ("b", upper)):
        go.arrive(f"s2{part}", f"o2{part}")
        merge(2, rows)
        go(f"att2{part}", att.at[2, rows, own_half], att.at[2, rows, own_half], cp)
    cross(EARLY, SPLIT)
    cross(SPLIT, 640)
    cross(640, WIDE)
    landed(5, owb.at[:, :, c])
    go.arrive_all("ow", owb.at[:, :, 1 - c], cp)
    go.arrive_all("att", att.at[0:2, :, own_half], cp)

    def project_two(dy, dx):
        return jnp.dot(
            jnp.concatenate([att[0], att[1]], axis=1),
            owb[chip(dy, dx), 0:2].reshape(4 * HD, OWN),
            preferred_element_type=F32,
        )

    def project_last(dy, dx, rows):
        return jnp.dot(
            att[2, rows, :], owb[chip(dy, dx), 2].reshape(2 * HD, OWN), preferred_element_type=F32
        )

    before, after, across = token_block(-1, 0), token_block(1, 0), token_block(2, 0)
    opposite = token_block(0, 1)
    before_opposite, after_opposite, across_opposite = token_block(-1, 1), token_block(1, 1), token_block(2, 1)

    def quarters(a):
        return a.reshape(2, 2, QUARTER, OWN)

    def send_far(dy, half):
        go(f"far+{dy}{half}", p_out.at[dy, half, 0], r_far.at[dy, half, 0], xp, f"far+{dy}")
        go(f"far-{dy}{half}", p_out.at[dy, half, 1], r_far.at[dy, half, 1], xm, f"far-{dy}")

    def far_block(dy, rows, half):
        out = p_far[dy, rows, :] + project_last(dy, 2, rows)
        p_out[dy, half] = out.astype(BF16).reshape(2, QUARTER, OWN)

    def near_blocks(dy):
        p_plus[dy] = quarters(project_two(dy, 1) + project_last(dy, 1, whole))
        y_out[0, dy, :, 1] = p_plus[dy, :, 1].astype(BF16)
        p_minus[dy] = quarters(project_two(dy, -1) + project_last(dy, -1, whole))
        y_out[1, dy, :, 0] = p_minus[dy, :, 0].astype(BF16)

    def send_early(dy):
        go(f"early+{dy}", y_out.at[0, dy, :, 1], r_plus.at[dy, :, 1], xp, f"plus{dy}")
        go(f"early-{dy}", y_out.at[1, dy, :, 0], r_minus.at[dy, :, 0], xm, f"minus{dy}")

    def add_far(dy):
        go.arrive_all(f"far+{dy}", r_far.at[dy, :, 0], xp)
        y_out[0, dy, :, 0] = (p_plus[dy, :, 0] + r_far[dy, :, 0].astype(F32)).astype(BF16)
        if dy == 1:
            go("late+1", y_out.at[0, 1, :, 0], r_plus.at[1, :, 0], xp, "plus1")
        else:
            for half in (0, 1):
                go(f"late+0{half}", y_out.at[0, 0, half, 0], r_plus.at[0, half, 0], xp)
        go.arrive_all(f"far-{dy}", r_far.at[dy, :, 1], xm)
        y_out[1, dy, :, 1] = (p_minus[dy, :, 1] + r_far[dy, :, 1].astype(F32)).astype(BF16)
        if dy == 1:
            go("late-1", y_out.at[1, 1, :, 1], r_minus.at[1, :, 1], xm, "minus1")
        else:
            for half in (0, 1):
                go(f"late-0{half}", y_out.at[1, 0, half, 1], r_minus.at[0, half, 1], xm)

    p_far[1] = project_two(1, 2)
    go.arrive("att2a")
    far_block(1, lower, 0)
    send_far(1, 0)
    go.arrive("att2b")
    far_block(1, upper, 1)
    send_far(1, 1)
    near_blocks(1)
    send_early(1)
    go.arrive("wz2+")
    part1, part2 = pl.ds(SPLIT, AHEAD), pl.ds(SPLIT + AHEAD, WIDE - SPLIT - AHEAD)
    go("wq1a", wb.at[before, part1], wb.at[before, part1], yp, "wq1")
    go.arrive("wz2-")
    go("wf2", wb.at[after, second], wb.at[after, second], zm)
    p_far[0] = project_two(0, 2)
    far_block(0, lower, 0)
    far_block(0, upper, 1)
    near_blocks(0)
    add_far(1)
    send_far(0, 0)
    send_far(0, 1)
    send_early(0)
    for dy in (1, 0):
        p_here[dy] = project_two(dy, 0) + project_last(dy, 0, whole)
    go.arrive_all("wy1", wb.at[opposite, first], yp)
    q1, q2 = pl.ds(0, SPLIT // 2), pl.ds(SPLIT // 2, SPLIT // 2)
    go("wp+a", wb.at[opposite, q1], wb.at[opposite, q1], zp)
    go.drain("n+2", "n-2", "f+1", "f-1", "f+2", "f-2", "s0", "o0", "s1", "o1", "att0", "att1")
    go.arrive_all("plus1", r_plus.at[1], xp)
    go.arrive_all("minus1", r_minus.at[1], xm)
    near = p_here[1] + (r_plus[1].astype(F32) + r_minus[1].astype(F32)).reshape(ROWS, OWN)
    y_in[0] = near.astype(BF16)
    go("rows", y_in.at[0], y_in.at[1], yq)
    go("wq1b", wb.at[before, part2], wb.at[before, part2], yp, "wq1")
    rows1, rows2 = pl.ds(0, WIDE // 2), pl.ds(WIDE // 2, SPLIT - WIDE // 2)
    go.arrive("wz1+")
    go("wf1", wb.at[before, rows1], wb.at[before, rows1], zp, "wf")
    go.arrive("wz1-")
    go("wf3", wb.at[after, rows2], wb.at[after, rows2], zm, "wf")
    go("wp-a", wb.at[opposite, q2], wb.at[opposite, q2], zm)
    go("wp+b", wb.at[opposite, q2], wb.at[opposite, q2], zp)
    go("wp-b", wb.at[opposite, q1], wb.at[opposite, q1], zm)
    add_far(0)
    landed(6, stream_vm)
    own, other_chip = chip(0, 0), chip(1, 0)

    def block(j, half=slice(None), way=slice(None)):
        return xb.at[j, half, way, :, mine]

    def spread(dy, half):
        j = chip(dy, 0)
        go(f"x+{dy}{half}", block(j, half), block(j, half), xp)
        go(f"x-{dy}{half}", block(j, half), block(j, half), xm)

    def pass_core(dy):
        left, right = chip(dy, -1), chip(dy, 1)
        go(f"xc+{dy}", block(left), block(left), cp)
        go(f"xc-{dy}", block(right), block(right), cp)

    go.arrive_all("plus0", r_plus.at[0, :, 1], xp)
    go.arrive_all("minus0", r_minus.at[0, :, 0], xm)
    for half, rows in ((0, lower), (1, upper)):
        go.arrive(f"late+0{half}", f"late-0{half}")
        if half == 0:
            go.arrive("rows")
        here = p_here[0, rows, :] + (r_plus[0, half].astype(F32) + r_minus[0, half].astype(F32)).reshape(HALF, OWN)
        here = here + stream_vm[rows].astype(F32) + y_in[1, rows].astype(F32)
        residual = here.astype(BF16)
        xb[own, half, :, :, mine] = residual.reshape(2, QUARTER, OWN)
        residual_ref[rows] = residual
        spread(0, half)
        go(f"xy{half}", block(own, half), block(own, half), yq)

    def prepare(j, start=False):
        gain = gain_ref[:, pl.ds(pl.multiple_of(j * WIDE, 128), WIDE)]
        level = xb[j].reshape(ROWS, WIDE).astype(F32)
        xg[j] = (level * gain).astype(BF16)
        level = level * level
        sums = level[:, 0:128]
        for k in range(1, WIDE // 128):
            sums = sums + level[:, k * 128 : (k + 1) * 128]
        squares[...] = sums if start else squares[...] + sums

    def expand(j, start=False):
        product = jnp.dot(xg[j], wb[j], preferred_element_type=F32)
        total[...] = product if start else total[...] + product

    go("xc", block(own), block(own), cp)
    go("wq2", wb.at[after, second], wb.at[after, second], yp)
    go.arrive("wf2")
    go("wq3", wb.at[across, second], wb.at[across, second], yp)
    go.drain(*[f"early{sign}{dy}" for sign in "+-" for dy in (0, 1)])
    go.drain(*[f"far{sign}{dy}{half}" for sign in "+-" for dy in (0, 1) for half in (0, 1)])
    go.drain("s2a", "o2a", "s2b", "o2b", "att2a", "att2b", *[f"wy{i}" for i in (0, 128, 256, EARLY, SPLIT, 640)])
    go.drain("wz2+", "wz2-", "wz1+", "wz1-", "late+1", "late-1")
    go.arrive("xy0")
    spread(1, 0)
    go.arrive("xc")
    prepare(own, start=True)
    go.arrive("xy1")
    spread(1, 1)
    go("xcy", block(other_chip), block(other_chip), cp)
    go.arrive("x+00", "x+01")
    go("xf+0", block(chip(0, -1), way=0), block(chip(0, -1), way=0), xp, "xf0")
    go.arrive("x-00", "x-01")
    go("xf-0", block(chip(0, 1), way=1), block(chip(0, 1), way=1), xm, "xf0")
    pass_core(0)
    go.arrive("wp+a")
    go("wpf+", wb.at[before_opposite, q1], wb.at[before_opposite, q1], zp, "wpf")
    go.arrive("wp-a")
    go("wpf-", wb.at[after_opposite, q2], wb.at[after_opposite, q2], zm, "wpf")
    go.arrive("xc+0")
    prepare(chip(0, -1))
    go.arrive("xc-0")
    prepare(chip(0, 1))
    go.arrive("xcy")
    prepare(other_chip)

    def pass_far(half):
        go.arrive(f"x+1{half}")
        go(f"xf+1{half}", block(chip(1, -1), half, 0), block(chip(1, -1), half, 0), xp, f"xf1{half}")
        go.arrive(f"x-1{half}")
        go(f"xf-1{half}", block(chip(1, 1), half, 1), block(chip(1, 1), half, 1), xm, f"xf1{half}")

    same = lax.rem(x + yh, 2)
    rest = 1 - same
    far_chip, last_chip = chip(0, 2), chip(1, 2)
    order = [
        chip(0, rest),
        jnp.where(same == 0, chip(0, 3), other_chip),
        chip(1, 1),
        chip(1, 3),
        far_chip,
    ]
    passed = order[0] == across_opposite
    turn = []
    for k in range(4):
        turn.append(jnp.where(passed, order[k + 1], order[k]))
        passed = passed | (order[k + 1] == across_opposite)
    turn.append(jnp.where(passed, across_opposite, order[4]))
    go.arrive_all("wf", wb.at[across, first], zp)
    expand(chip(0, same), start=True)
    pass_far(0)
    expand(jnp.where(same == 0, other_chip, chip(0, 3)))
    pass_far(1)
    pass_core(1)
    go.arrive("xc+1")
    prepare(chip(1, -1))
    go.arrive("xc-1")
    prepare(chip(1, 1))
    go.arrive_all("wy2", wb.at[opposite, second], yp)
    go.arrive_all("wq1", wb.at[before_opposite, second], yp)
    go.arrive("wp+b", "wp-b", "wq2")
    expand(turn[0])
    expand(turn[1])
    expand(turn[2])
    go.arrive_all("xf0", block(far_chip), xp)
    go("xcf0", block(far_chip), block(far_chip), cp)
    go.arrive("xcf0")
    prepare(far_chip)
    go.arrive_all("xf10", block(last_chip, 0), xp)
    go("xcf10", block(last_chip, 0), block(last_chip, 0), cp)
    expand(turn[3])
    go.arrive_all("xf11", block(last_chip, 1), xp)
    go("xcf11", block(last_chip, 1), block(last_chip, 1), cp)
    go.arrive("wq3")
    go.arrive_all("wpf", wb.at[across_opposite, first], zp)
    expand(turn[4])
    gain = gain_ref[:, pl.ds(pl.multiple_of(last_chip * WIDE, 128), WIDE)]
    for half, rows in ((0, lower), (1, upper)):
        go.arrive(f"xcf1{half}")
        level = xb[last_chip, half].reshape(HALF, WIDE).astype(F32)
        product = jnp.dot((level * gain).astype(BF16), wb[last_chip], preferred_element_type=F32)
        square = jnp.sum(level * level, axis=1, keepdims=True) + jnp.sum(squares[rows], axis=1, keepdims=True)
        inverse = lax.rsqrt(square * (1.0 / D) + 1e-6)
        expanded_ref[rows] = jax.nn.gelu((total[rows] + product) * inverse, approximate=True).astype(BF16)
    go.drain()
    assert go.used <= N_SEND and len(go.groups) <= N_RECV, (go.used, len(go.groups))


def body(queries, keys, values, stream, out_weight, norm_gain, up_weight):
    anywhere = pl.BlockSpec(memory_space=pl.ANY)
    vmem = pl.BlockSpec(memory_space=pltpu.VMEM)
    return pl.pallas_call(
        kernel,
        out_shape=(
            pltpu.VMEM((ROWS, OWN), BF16),
            pltpu.VMEM((ROWS, WIDE), BF16),
        ),
        in_specs=[anywhere, anywhere, anywhere, anywhere, anywhere, vmem, anywhere],
        out_specs=(vmem, vmem),
        scratch_shapes=[
            pltpu.VMEM((2, 3, ROWS, HD), BF16),
            pltpu.VMEM((3, 4, 2, ROWS, HD), BF16),
            pltpu.VMEM((3, ROWS, HD), BF16),
            pltpu.VMEM((3, 8, ROWS), F32),
            pltpu.VMEM((3, ROWS, HD), BF16),
            pltpu.VMEM((3, 8, ROWS), F32),
            pltpu.VMEM((2, 3, ROWS, HD), F32),
            pltpu.VMEM((2, 3, ROWS, HD), F32),
            pltpu.VMEM((3, ROWS, 2 * HD), BF16),
            pltpu.VMEM((8, 3, 2, HD, OWN), BF16),
            pltpu.VMEM((8, WIDE, WIDE), BF16),
            pltpu.VMEM((ROWS, OWN), BF16),
            pltpu.VMEM((2, ROWS, OWN), F32),
            pltpu.VMEM((2, 2, 2, QUARTER, OWN), BF16),
            pltpu.VMEM((2, 2, 2, QUARTER, OWN), F32),
            pltpu.VMEM((2, 2, 2, QUARTER, OWN), F32),
            pltpu.VMEM((2, ROWS, OWN), F32),
            pltpu.VMEM((2, 2, 2, QUARTER, OWN), BF16),
            pltpu.VMEM((2, 2, 2, QUARTER, OWN), BF16),
            pltpu.VMEM((2, 2, 2, QUARTER, OWN), BF16),
            pltpu.VMEM((2, 2, 2, 2, QUARTER, OWN), BF16),
            pltpu.VMEM((2, ROWS, OWN), BF16),
            pltpu.VMEM((8, 2, 2, QUARTER, WIDE), BF16),
            pltpu.VMEM((8, ROWS, WIDE), BF16),
            pltpu.VMEM((ROWS, WIDE), F32),
            pltpu.VMEM((ROWS, 128), F32),
            pltpu.SemaphoreType.DMA((N_SEND,)),
            pltpu.SemaphoreType.DMA((N_RECV,)),
            pltpu.SemaphoreType.DMA((N_LOCAL,)),
        ],
        compiler_params=pltpu.CompilerParams(
            collective_id=0, has_side_effects=True, vmem_limit_bytes=53 * 2**20
        ),
        cost_estimate=pl.CostEstimate(flops=10_500_000_000, bytes_accessed=12_000_000, transcendentals=6_300_000),
    )(queries, keys, values, stream, out_weight.reshape(3, HD, D), norm_gain.reshape(1, D), up_weight)


def solution(mesh):
    in_specs = (
        P("seq", "tensor"),
        P("seq", "tensor"),
        P("seq", "tensor"),
        P("seq", "tensor"),
        P("tensor", None),
        P(),
        P("seq", "tensor"),
    )
    out_specs = (P("seq", "tensor"), P("seq", "tensor"))
    return jax.shard_map(body, mesh=mesh, in_specs=in_specs, out_specs=out_specs, check_vma=False)
```

```python
import math

import jax
import jax.numpy as jnp
from jax import lax
from jax.experimental import pallas as pl
from jax.experimental.pallas import tpu as pltpu
from jax.sharding import PartitionSpec as P

D = 6144
HD = 128
EXPONENT = math.log2(math.e) / math.sqrt(HD)
MESH = pl.DeviceIdType.MESH
BF16 = jnp.bfloat16
F32 = jnp.float32

ROWS = 512
HALF = 256
QUARTER = 128
OWN = 384
WIDE = 768
SPLIT = 512


class Copies:
    def __init__(self, send, recv):
        self.send, self.recv = send, recv
        self.made, self.slots, self.groups = {}, {}, {}
        self.free, self.used = [], 0

    def __call__(self, name, src, dst, device, group=None):
        if not self.free:
            self.free.append(self.used)
            self.used += 1
        self.slots[name] = slot = self.free.pop()
        index = self.groups.setdefault(group or name, len(self.groups))
        self.made[name] = copy = pltpu.make_async_remote_copy(
            src_ref=src,
            dst_ref=dst,
            send_sem=self.send.at[slot],
            recv_sem=self.recv.at[index],
            device_id=device,
            device_id_type=MESH,
        )
        copy.start()

    def arrive(self, *names):
        for name in names:
            self.made[name].wait_recv()

    def arrive_all(self, group, ref, device):
        pltpu.make_async_remote_copy(
            src_ref=ref,
            dst_ref=ref,
            send_sem=self.send.at[0],
            recv_sem=self.recv.at[self.groups[group]],
            device_id=device,
            device_id_type=MESH,
        ).wait_recv()

    def drain(self, *names):
        for name in names or tuple(self.slots):
            self.made[name].wait_send()
            self.free.append(self.slots.pop(name))


N_SEND = 54
EARLY = 384
AHEAD = 160
N_RECV = 75
N_LOCAL = 8


def kernel(
    q_ref, k_ref, v_ref, stream_ref, ow_ref, gain_ref, up_ref,
    residual_ref, expanded_ref,
    qb, kvb, o_out, st_out, o_in, st_in, o_part, st_part, att, owb, wb, stream_vm,
    p_far, p_out, p_plus, p_minus, p_here, r_far, r_plus, r_minus, y_out, y_in, xb, xg, total, squares,
    send, recv, local_sem,
):
    s = lax.axis_index("seq")
    t = lax.axis_index("tensor")
    z, yh = s // 2, lax.rem(s, 2)
    yl, x, c = t // 8, lax.rem(t // 2, 4), lax.rem(t, 2)

    def ring(a, d):
        return lax.rem(a + d + 4, 4)

    def token_block(dz, dy):
        return ring(z, dz) * 2 + (yh if dy == 0 else 1 - yh)

    def chip(dy, dx):
        return (yl if dy == 0 else 1 - yl) * 4 + ring(x, dx)

    zp, zm = (token_block(1, 0), t), (token_block(-1, 0), t)
    yp = (token_block(0, 1), t)
    xp, xm = (s, chip(0, 1) * 2 + c), (s, chip(0, -1) * 2 + c)
    yq = (s, chip(1, 0) * 2 + c)
    cp = (s, chip(0, 0) * 2 + 1 - c)
    partners = (zp, zm, yp, xp, xm, yq, cp)

    barrier = pltpu.get_barrier_semaphore()
    for device in partners:
        pl.semaphore_signal(barrier, inc=1, device_id=device, device_id_type=MESH)

    def local(index, *pairs):
        for src, dst in pairs:
            pltpu.make_async_copy(src, dst, local_sem.at[index]).start()

    def landed(index, ref):
        pltpu.make_async_copy(ref, ref, local_sem.at[index]).wait()

    def head_columns(h):
        return pl.ds(h * HD, HD)

    for h in range(3):
        local(
            h,
            (k_ref.at[:, head_columns(h)], kvb.at[h, 0, 0]),
            (v_ref.at[:, head_columns(h)], kvb.at[h, 0, 1]),
        )
    local(3, *[(q_ref.at[:, head_columns(h)], qb.at[0, h]) for h in range(3)])
    local(4, (up_ref, wb.at[s]))
    mine = pl.ds(pl.multiple_of(c * OWN, 128), OWN)

    def feature_block(j, core):
        return pl.ds(pl.multiple_of((2 * j + core) * OWN, 128), OWN)

    local(5, *[(ow_ref.at[:, :, feature_block(j, c)], owb.at[j, :, c]) for j in range(8)])
    local(6, (stream_ref, stream_vm))

    def greeted():
        pl.semaphore_wait(barrier, len(partners))

    greeted()
    go = Copies(send, recv)

    lower, upper = pl.ds(0, HALF), pl.ds(HALF, HALF)

    def near(h):
        go(f"n+{h}", kvb.at[h, 0], kvb.at[h, 1], zp)
        go(f"n-{h}", kvb.at[h, 0], kvb.at[h, 2], zm)

    def far(h):
        go.arrive(f"n+{h}")
        go(f"f+{h}", kvb.at[h, 1, :, lower], kvb.at[h, 3, :, lower], zp, f"f{h}")
        go.arrive(f"n-{h}")
        go(f"f-{h}", kvb.at[h, 2, :, upper], kvb.at[h, 3, :, upper], zm, f"f{h}")

    def scores_of(which, h, rows, slots):
        keys = kvb[h, slots, 0].reshape(-1, HD)
        return lax.dot_general(
            qb[which, h, rows, :], keys, (((1,), (1,)), ((), ())), preferred_element_type=F32
        )

    lane = lax.broadcasted_iota(jnp.int32, (HALF, HD), 1)

    def attend_near(which, h):
        def tile(i, carry):
            rows = pl.ds(pl.multiple_of(i * HALF, HALF), HALF)
            slots = slice(0, 3)
            scores = scores_of(which, h, rows, slots)
            top = jnp.max(scores, axis=1, keepdims=True)
            weights = jnp.exp2((scores - top) * EXPONENT)
            bottom = jnp.sum(weights, axis=1, keepdims=True)
            o_part[which, h, rows, :] = jnp.dot(
                weights.astype(BF16), kvb[h, slots, 1].reshape(-1, HD), preferred_element_type=F32
            )
            st_part[which, h, rows, :] = jnp.where(lane == 0, top, bottom)
            return carry

        lax.fori_loop(0, 2, tile, 0)

    def attend_far(which, h, halves=None):
        def tile(i, carry):
            rows = pl.ds(i * HALF if isinstance(i, int) else pl.multiple_of(i * HALF, HALF), HALF)
            slots = slice(3, 4)
            scores = scores_of(which, h, rows, slots)
            stats = st_part[which, h, rows, :]
            top_near, bottom_near = stats[:, 0:1], stats[:, 1:2]
            top = jnp.maximum(top_near, jnp.max(scores, axis=1, keepdims=True))
            weights = jnp.exp2((scores - top) * EXPONENT)
            decay = jnp.exp2((top_near - top) * EXPONENT)
            bottom = bottom_near * decay + jnp.sum(weights, axis=1, keepdims=True)
            out = jnp.dot(weights.astype(BF16), kvb[h, slots, 1].reshape(-1, HD), preferred_element_type=F32)
            out = (o_part[which, h, rows, :] * decay + out) / bottom
            both = jnp.where(lane == 0, top, bottom)
            if which == 1:
                o_out[h, rows, :] = out.astype(BF16)
                st_out[h, :, rows] = both.T[:8]
            else:
                o_part[0, h, rows, :] = out
                st_part[0, h, rows, :] = both
            return carry

        if halves is None:
            lax.fori_loop(0, 2, tile, 0)
        else:
            tile(halves, 0)

    def give_back(h, part="", rows=slice(None)):
        go(f"s{h}{part}", st_out.at[h, :, rows], st_in.at[h, :, rows], yp)
        go(f"o{h}{part}", o_out.at[h, rows], o_in.at[h, rows], yp)

    landed(0, kvb.at[0, 0])
    near(0)
    landed(1, kvb.at[1, 0])
    near(1)
    landed(3, qb.at[0])
    for h in range(3):
        go(f"q{h}", qb.at[0, h], qb.at[1, h], yp)
    for j in range(8):
        go(f"ow{j}", ow_ref.at[:, :, feature_block(j, 1 - c)], owb.at[j, :, c], cp, "ow")
    landed(2, kvb.at[2, 0])
    landed(4, wb.at[s])
    first, second = pl.ds(0, SPLIT), pl.ds(SPLIT, WIDE - SPLIT)
    own_rows = token_block(0, 0)

    def cross(start, stop):
        rows = pl.ds(start, stop - start)
        go(f"wy{start}", wb.at[own_rows, rows], wb.at[own_rows, rows], yp, "wy1" if start < SPLIT else "wy2")

    cross(0, 128)
    cross(128, 256)
    far(0)
    near(2)
    go.arrive("q0")
    attend_near(1, 0)
    attend_near(0, 0)
    far(1)
    go.arrive("q1")
    attend_near(1, 1)
    attend_near(0, 1)
    go.arrive_all("f0", kvb.at[0, 3], zp)
    attend_far(1, 0)
    give_back(0)
    cross(256, EARLY)
    attend_far(0, 0)
    far(2)
    go.arrive("q2")
    attend_near(1, 2)
    attend_near(0, 2)
    go("wz2+", wb.at[own_rows, second], wb.at[own_rows, second], zp)
    go("wz2-", wb.at[own_rows, second], wb.at[own_rows, second], zm)
    go("wz1+", wb.at[own_rows, first], wb.at[own_rows, first], zp)
    go("wz1-", wb.at[own_rows, first], wb.at[own_rows, first], zm)
    go.arrive_all("f1", kvb.at[1, 3], zp)
    attend_far(1, 1)
    give_back(1)
    go.arrive_all("f2", kvb.at[2, 3], zp)
    attend_far(1, 2, 0)
    give_back(2, "a", lower)
    attend_far(1, 2, 1)
    give_back(2, "b", upper)
    attend_far(0, 1)
    attend_far(0, 2)

    def merge(h, rows):
        theirs = jnp.concatenate([st_in[h, :, rows]] * 16, axis=0).T
        ours = st_part[0, h, rows, :]
        top1, sum1 = ours[:, 0:1], ours[:, 1:2]
        top2, sum2 = theirs[:, 0:1], theirs[:, 1:2]
        top = jnp.maximum(top1, top2)
        w1 = sum1 * jnp.exp2((top1 - top) * EXPONENT)
        w2 = sum2 * jnp.exp2((top2 - top) * EXPONENT)
        scale = 1.0 / (w1 + w2)
        merged = (w1 * scale) * o_part[0, h, rows, :] + (w2 * scale) * o_in[h, rows, :].astype(F32)
        att[h, rows, own_half] = merged.astype(BF16)

    own_half = pl.ds(pl.multiple_of(c * HD, HD), HD)
    whole = pl.ds(0, ROWS)
    for h in range(2):
        go.arrive(f"s{h}", f"o{h}")
        merge(h, whole)
        go(f"att{h}", att.at[h, :, own_half], att.at[h, :, own_half], cp, "att")
    go.drain(*[f"{kind}{h}" for kind in ("n+", "n-") for h in range(2)], "f+0", "f-0", "q0", "q1", "q2")
    go.drain(*[f"ow{j}" for j in range(8)])
    for part, rows in (("a", lower), ("b", upper)):
        go.arrive(f"s2{part}", f"o2{part}")
        merge(2, rows)
        go(f"att2{part}", att.at[2, rows, own_half], att.at[2, rows, own_half], cp)
    cross(EARLY, SPLIT)
    cross(SPLIT, 640)
    cross(640, WIDE)
    landed(5, owb.at[:, :, c])
    go.arrive_all("ow", owb.at[:, :, 1 - c], cp)
    go.arrive_all("att", att.at[0:2, :, own_half], cp)

    def project_two(dy, dx):
        return jnp.dot(
            jnp.concatenate([att[0], att[1]], axis=1),
            owb[chip(dy, dx), 0:2].reshape(4 * HD, OWN),
            preferred_element_type=F32,
        )

    def project_last(dy, dx, rows):
        return jnp.dot(
            att[2, rows, :], owb[chip(dy, dx), 2].reshape(2 * HD, OWN), preferred_element_type=F32
        )

    before, after, across = token_block(-1, 0), token_block(1, 0), token_block(2, 0)
    opposite = token_block(0, 1)
    before_opposite, after_opposite, across_opposite = token_block(-1, 1), token_block(1, 1), token_block(2, 1)

    def quarters(a):
        return a.reshape(2, 2, QUARTER, OWN)

    def send_far(dy, half):
        go(f"far+{dy}{half}", p_out.at[dy, half, 0], r_far.at[dy, half, 0], xp, f"far+{dy}")
        go(f"far-{dy}{half}", p_out.at[dy, half, 1], r_far.at[dy, half, 1], xm, f"far-{dy}")

    def far_block(dy, rows, half):
        out = p_far[dy, rows, :] + project_last(dy, 2, rows)
        p_out[dy, half] = out.astype(BF16).reshape(2, QUARTER, OWN)

    def near_blocks(dy):
        p_plus[dy] = quarters(project_two(dy, 1) + project_last(dy, 1, whole))
        y_out[0, dy, :, 1] = p_plus[dy, :, 1].astype(BF16)
        p_minus[dy] = quarters(project_two(dy, -1) + project_last(dy, -1, whole))
        y_out[1, dy, :, 0] = p_minus[dy, :, 0].astype(BF16)

    def send_early(dy):
        go(f"early+{dy}", y_out.at[0, dy, :, 1], r_plus.at[dy, :, 1], xp, f"plus{dy}")
        go(f"early-{dy}", y_out.at[1, dy, :, 0], r_minus.at[dy, :, 0], xm, f"minus{dy}")

    def add_far(dy):
        go.arrive_all(f"far+{dy}", r_far.at[dy, :, 0], xp)
        y_out[0, dy, :, 0] = (p_plus[dy, :, 0] + r_far[dy, :, 0].astype(F32)).astype(BF16)
        if dy == 1:
            go("late+1", y_out.at[0, 1, :, 0], r_plus.at[1, :, 0], xp, "plus1")
        else:
            for half in (0, 1):
                go(f"late+0{half}", y_out.at[0, 0, half, 0], r_plus.at[0, half, 0], xp)
        go.arrive_all(f"far-{dy}", r_far.at[dy, :, 1], xm)
        y_out[1, dy, :, 1] = (p_minus[dy, :, 1] + r_far[dy, :, 1].astype(F32)).astype(BF16)
        if dy == 1:
            go("late-1", y_out.at[1, 1, :, 1], r_minus.at[1, :, 1], xm, "minus1")
        else:
            for half in (0, 1):
                go(f"late-0{half}", y_out.at[1, 0, half, 1], r_minus.at[0, half, 1], xm)

    p_far[1] = project_two(1, 2)
    go.arrive("att2a")
    far_block(1, lower, 0)
    send_far(1, 0)
    go.arrive("att2b")
    far_block(1, upper, 1)
    send_far(1, 1)
    near_blocks(1)
    send_early(1)
    go.arrive("wz2+")
    part1, part2 = pl.ds(SPLIT, AHEAD), pl.ds(SPLIT + AHEAD, WIDE - SPLIT - AHEAD)
    go("wq1a", wb.at[before, part1], wb.at[before, part1], yp, "wq1")
    go.arrive("wz2-")
    go("wf2", wb.at[after, second], wb.at[after, second], zm)
    p_far[0] = project_two(0, 2)
    far_block(0, lower, 0)
    far_block(0, upper, 1)
    near_blocks(0)
    add_far(1)
    send_far(0, 0)
    send_far(0, 1)
    send_early(0)
    for dy in (1, 0):
        p_here[dy] = project_two(dy, 0) + project_last(dy, 0, whole)
    go.arrive_all("wy1", wb.at[opposite, first], yp)
    q1, q2 = pl.ds(0, SPLIT // 2), pl.ds(SPLIT // 2, SPLIT // 2)
    go("wp+a", wb.at[opposite, q1], wb.at[opposite, q1], zp)
    go.drain("n+2", "n-2", "f+1", "f-1", "f+2", "f-2", "s0", "o0", "s1", "o1", "att0", "att1")
    go.arrive_all("plus1", r_plus.at[1], xp)
    go.arrive_all("minus1", r_minus.at[1], xm)
    near = p_here[1] + (r_plus[1].astype(F32) + r_minus[1].astype(F32)).reshape(ROWS, OWN)
    y_in[0] = near.astype(BF16)
    go("rows", y_in.at[0], y_in.at[1], yq)
    go("wq1b", wb.at[before, part2], wb.at[before, part2], yp, "wq1")
    rows1, rows2 = pl.ds(0, WIDE // 2), pl.ds(WIDE // 2, SPLIT - WIDE // 2)
    go.arrive("wz1+")
    go("wf1", wb.at[before, rows1], wb.at[before, rows1], zp, "wf")
    go.arrive("wz1-")
    go("wf3", wb.at[after, rows2], wb.at[after, rows2], zm, "wf")
    go("wp-a", wb.at[opposite, q2], wb.at[opposite, q2], zm)
    go("wp+b", wb.at[opposite, q2], wb.at[opposite, q2], zp)
    go("wp-b", wb.at[opposite, q1], wb.at[opposite, q1], zm)
    add_far(0)
    landed(6, stream_vm)
    own, other_chip = chip(0, 0), chip(1, 0)

    def block(j, half=slice(None), way=slice(None)):
        return xb.at[j, half, way, :, mine]

    def spread(dy, half):
        j = chip(dy, 0)
        go(f"x+{dy}{half}", block(j, half), block(j, half), xp)
        go(f"x-{dy}{half}", block(j, half), block(j, half), xm)

    def pass_core(dy):
        left, right = chip(dy, -1), chip(dy, 1)
        go(f"xc+{dy}", block(left), block(left), cp)
        go(f"xc-{dy}", block(right), block(right), cp)

    go.arrive_all("plus0", r_plus.at[0, :, 1], xp)
    go.arrive_all("minus0", r_minus.at[0, :, 0], xm)
    for half, rows in ((0, lower), (1, upper)):
        go.arrive(f"late+0{half}", f"late-0{half}")
        if half == 0:
            go.arrive("rows")
        here = p_here[0, rows, :] + (r_plus[0, half].astype(F32) + r_minus[0, half].astype(F32)).reshape(HALF, OWN)
        here = here + stream_vm[rows].astype(F32) + y_in[1, rows].astype(F32)
        residual = here.astype(BF16)
        xb[own, half, :, :, mine] = residual.reshape(2, QUARTER, OWN)
        residual_ref[rows] = residual
        spread(0, half)
        go(f"xy{half}", block(own, half), block(own, half), yq)

    def prepare(j, start=False):
        gain = gain_ref[:, pl.ds(pl.multiple_of(j * WIDE, 128), WIDE)]
        level = xb[j].reshape(ROWS, WIDE).astype(F32)
        xg[j] = (level * gain).astype(BF16)
        level = level * level
        sums = level[:, 0:128]
        for k in range(1, WIDE // 128):
            sums = sums + level[:, k * 128 : (k + 1) * 128]
        squares[...] = sums if start else squares[...] + sums

    def expand(j, start=False):
        product = jnp.dot(xg[j], wb[j], preferred_element_type=F32)
        total[...] = product if start else total[...] + product

    def expand_two(j, k):
        total[...] += jnp.dot(
            jnp.concatenate([xg[j], xg[k]], axis=1),
            jnp.concatenate([wb[j], wb[k]], axis=0),
            preferred_element_type=F32,
        )

    go("xc", block(own), block(own), cp)
    go("wq2", wb.at[after, second], wb.at[after, second], yp)
    go.arrive("wf2")
    go("wq3", wb.at[across, second], wb.at[across, second], yp)
    go.drain(*[f"early{sign}{dy}" for sign in "+-" for dy in (0, 1)])
    go.drain(*[f"far{sign}{dy}{half}" for sign in "+-" for dy in (0, 1) for half in (0, 1)])
    go.drain("s2a", "o2a", "s2b", "o2b", "att2a", "att2b", *[f"wy{i}" for i in (0, 128, 256, EARLY, SPLIT, 640)])
    go.drain("wz2+", "wz2-", "wz1+", "wz1-", "late+1", "late-1")
    go.arrive("xy0")
    spread(1, 0)
    go.arrive("xc")
    prepare(own, start=True)
    go.arrive("xy1")
    spread(1, 1)
    go("xcy", block(other_chip), block(other_chip), cp)
    go.arrive("x+00", "x+01")
    go("xf+0", block(chip(0, -1), way=0), block(chip(0, -1), way=0), xp, "xf0")
    go.arrive("x-00", "x-01")
    go("xf-0", block(chip(0, 1), way=1), block(chip(0, 1), way=1), xm, "xf0")
    pass_core(0)
    go.arrive("wp+a")
    go("wpf+", wb.at[before_opposite, q1], wb.at[before_opposite, q1], zp, "wpf")
    go.arrive("wp-a")
    go("wpf-", wb.at[after_opposite, q2], wb.at[after_opposite, q2], zm, "wpf")
    go.arrive("xc+0")
    prepare(chip(0, -1))
    go.arrive("xc-0")
    prepare(chip(0, 1))
    go.arrive("xcy")
    prepare(other_chip)

    def pass_far(half):
        go.arrive(f"x+1{half}")
        go(f"xf+1{half}", block(chip(1, -1), half, 0), block(chip(1, -1), half, 0), xp, f"xf1{half}")
        go.arrive(f"x-1{half}")
        go(f"xf-1{half}", block(chip(1, 1), half, 1), block(chip(1, 1), half, 1), xm, f"xf1{half}")

    same = lax.rem(x + yh, 2)
    rest = 1 - same
    far_chip, last_chip = chip(0, 2), chip(1, 2)
    order = [
        chip(0, rest),
        jnp.where(same == 0, chip(0, 3), other_chip),
        chip(1, 1),
        chip(1, 3),
        far_chip,
    ]
    passed = order[0] == across_opposite
    turn = []
    for k in range(4):
        turn.append(jnp.where(passed, order[k + 1], order[k]))
        passed = passed | (order[k + 1] == across_opposite)
    turn.append(jnp.where(passed, across_opposite, order[4]))
    go.arrive_all("wf", wb.at[across, first], zp)
    expand(chip(0, same), start=True)
    pass_far(0)
    expand(jnp.where(same == 0, other_chip, chip(0, 3)))
    pass_far(1)
    pass_core(1)
    go.arrive("xc+1")
    prepare(chip(1, -1))
    go.arrive("xc-1")
    prepare(chip(1, 1))
    go.arrive_all("wy2", wb.at[opposite, second], yp)
    go.arrive_all("wq1", wb.at[before_opposite, second], yp)
    go.arrive("wp+b", "wp-b", "wq2")
    expand_two(turn[0], turn[1])
    expand(turn[2])
    go.arrive_all("xf0", block(far_chip), xp)
    go("xcf0", block(far_chip), block(far_chip), cp)
    go.arrive("xcf0")
    prepare(far_chip)
    go.arrive_all("xf10", block(last_chip, 0), xp)
    go("xcf10", block(last_chip, 0), block(last_chip, 0), cp)
    expand(turn[3])
    go.arrive_all("xf11", block(last_chip, 1), xp)
    go("xcf11", block(last_chip, 1), block(last_chip, 1), cp)
    go.arrive("wq3")
    go.arrive_all("wpf", wb.at[across_opposite, first], zp)
    expand(turn[4])
    gain = gain_ref[:, pl.ds(pl.multiple_of(last_chip * WIDE, 128), WIDE)]
    for half, rows in ((0, lower), (1, upper)):
        go.arrive(f"xcf1{half}")
        level = xb[last_chip, half].reshape(HALF, WIDE).astype(F32)
        product = jnp.dot((level * gain).astype(BF16), wb[last_chip], preferred_element_type=F32)
        square = jnp.sum(level * level, axis=1, keepdims=True) + jnp.sum(squares[rows], axis=1, keepdims=True)
        inverse = lax.rsqrt(square * (1.0 / D) + 1e-6)
        expanded_ref[rows] = jax.nn.gelu((total[rows] + product) * inverse, approximate=True).astype(BF16)
    go.drain()
    assert go.used <= N_SEND and len(go.groups) <= N_RECV, (go.used, len(go.groups))


def body(queries, keys, values, stream, out_weight, norm_gain, up_weight):
    anywhere = pl.BlockSpec(memory_space=pl.ANY)
    vmem = pl.BlockSpec(memory_space=pltpu.VMEM)
    return pl.pallas_call(
        kernel,
        out_shape=(
            pltpu.VMEM((ROWS, OWN), BF16),
            pltpu.VMEM((ROWS, WIDE), BF16),
        ),
        in_specs=[anywhere, anywhere, anywhere, anywhere, anywhere, vmem, anywhere],
        out_specs=(vmem, vmem),
        scratch_shapes=[
            pltpu.VMEM((2, 3, ROWS, HD), BF16),
            pltpu.VMEM((3, 4, 2, ROWS, HD), BF16),
            pltpu.VMEM((3, ROWS, HD), BF16),
            pltpu.VMEM((3, 8, ROWS), F32),
            pltpu.VMEM((3, ROWS, HD), BF16),
            pltpu.VMEM((3, 8, ROWS), F32),
            pltpu.VMEM((2, 3, ROWS, HD), F32),
            pltpu.VMEM((2, 3, ROWS, HD), F32),
            pltpu.VMEM((3, ROWS, 2 * HD), BF16),
            pltpu.VMEM((8, 3, 2, HD, OWN), BF16),
            pltpu.VMEM((8, WIDE, WIDE), BF16),
            pltpu.VMEM((ROWS, OWN), BF16),
            pltpu.VMEM((2, ROWS, OWN), F32),
            pltpu.VMEM((2, 2, 2, QUARTER, OWN), BF16),
            pltpu.VMEM((2, 2, 2, QUARTER, OWN), F32),
            pltpu.VMEM((2, 2, 2, QUARTER, OWN), F32),
            pltpu.VMEM((2, ROWS, OWN), F32),
            pltpu.VMEM((2, 2, 2, QUARTER, OWN), BF16),
            pltpu.VMEM((2, 2, 2, QUARTER, OWN), BF16),
            pltpu.VMEM((2, 2, 2, QUARTER, OWN), BF16),
            pltpu.VMEM((2, 2, 2, 2, QUARTER, OWN), BF16),
            pltpu.VMEM((2, ROWS, OWN), BF16),
            pltpu.VMEM((8, 2, 2, QUARTER, WIDE), BF16),
            pltpu.VMEM((8, ROWS, WIDE), BF16),
            pltpu.VMEM((ROWS, WIDE), F32),
            pltpu.VMEM((ROWS, 128), F32),
            pltpu.SemaphoreType.DMA((N_SEND,)),
            pltpu.SemaphoreType.DMA((N_RECV,)),
            pltpu.SemaphoreType.DMA((N_LOCAL,)),
        ],
        compiler_params=pltpu.CompilerParams(
            collective_id=0, has_side_effects=True, vmem_limit_bytes=53 * 2**20
        ),
        cost_estimate=pl.CostEstimate(flops=10_500_000_000, bytes_accessed=12_000_000, transcendentals=6_300_000),
    )(queries, keys, values, stream, out_weight.reshape(3, HD, D), norm_gain.reshape(1, D), up_weight)


def solution(mesh):
    in_specs = (
        P("seq", "tensor"),
        P("seq", "tensor"),
        P("seq", "tensor"),
        P("seq", "tensor"),
        P("tensor", None),
        P(),
        P("seq", "tensor"),
    )
    out_specs = (P("seq", "tensor"), P("seq", "tensor"))
    return jax.shard_map(body, mesh=mesh, in_specs=in_specs, out_specs=out_specs, check_vma=False)
```
